256 devices in a mesh: store: 16 (over z, core), cand: 16 (over x, y).
Axes of the slice: x: 4, y: 4, z: 8, core: 2. Of those that a mesh axis runs over, the one named last changes fastest.
Arguments:
- kv_cache: bfloat16 [256, 2, 1024, 2048], P('store', None, 'cand'), may hold values from -6 to 6
- requests: int32 [256], P('store'), may hold values from 0 to 15, as said below
- lengths: int32 [256], P('store'), may hold values from 128 to 1024, as said below
- cand_feats: bfloat16 [256, 384, 1024], P('store', 'cand'), may hold values from -6 to 6
- w_in: bfloat16 [2, 1024, 4096], P(None, None, 'cand'), may hold values from -0.1875 to 0.1875
- w_out: bfloat16 [2, 1024, 1024], P(None, None, 'cand'), may hold values from -0.1875 to 0.1875
Outputs:
- ranked: bfloat16 [256, 384, 1024], P('store', 'cand')
The draws below stay inside these ranges and needn't reach their ends.
Inputs may be any that keep to these rules, and one draw needn't show every extreme that they name: `requests`: among the 16 users of one store index, every scorer index appears exactly 1 times. `lengths`: multiples of 128; some slot has 1024.
All inputs are finite; a program needn't handle non-finite values.
Results may differ from the reference program's by a relative error of at most 0.011.
Values may be sent and summed in bfloat16 or wider, within the bound.
A program may use at most 128 MiB of HBM per device.

```python
import jax
import jax.numpy as jnp
from jax import lax

D = 1024
HEADS = 8
HEAD = 128
LAYERS = 2
BLOCK = 128
PER_PAIR = 1
U_OWN = 16
USERS = 256
HIST = 1024
CANDS = 384
N_STORE = 16


def draw_requests(key, part):
    key = jax.random.fold_in(key, 11)
    owners = USERS // U_OWN
    base = jnp.arange(U_OWN, dtype=jnp.int32) // PER_PAIR
    keys = jax.random.split(key, owners)
    table = jax.vmap(lambda single: jax.random.permutation(single, base))(keys)
    return table.reshape(USERS).astype(jnp.int32)


def draw_lengths(key, part):
    key = jax.random.fold_in(key, 23)
    first, second = jax.random.split(key)
    blocks = jax.random.randint(first, (USERS,), 1, HIST // BLOCK + 1, dtype=jnp.int32)
    fullest = jax.random.randint(second, (), 0, USERS, dtype=jnp.int32)
    blocks = jnp.where(jnp.arange(USERS, dtype=jnp.int32) == fullest, HIST // BLOCK, blocks)
    return (blocks * BLOCK).astype(jnp.int32)


def shard_levels(stream_key, extent, cuts, least, largest):
    def one(dim, shards_of):
        heights = jax.random.uniform(jax.random.fold_in(jax.random.fold_in(stream_key, 6), dim), (shards_of,), jnp.float32, least / len(cuts), largest / len(cuts))
        return jnp.repeat(jnp.exp(heights), extent[dim] // shards_of).reshape((-1,) + (1,) * (len(extent) - dim - 1))

    loudness = one(*cuts[0])
    for cut in cuts[1:]:
        loudness = loudness * one(*cut)
    return loudness


def scatter_about(stream_key, extent, width, most, pieces=(), kind=jnp.bfloat16):
    result = jax.random.normal(stream_key, extent, jnp.float32) * width
    if len(pieces) > 0:
        result = shard_levels(stream_key, extent, pieces, -0.22, 0.18) * result
    return jnp.clip(result, min=-most, max=most).astype(kind)


def setup_inputs(seed: int = 0) -> dict:
    key_of = jax.random.split(jax.random.key(seed), 7)
    kv_cache = scatter_about(key_of[0], (USERS, LAYERS, HIST, 2 * D), 1.0, 6.0, ((0, 16), (2, 16)))
    requests = draw_requests(jax.random.fold_in(key_of[6], 71), 0)
    lengths = draw_lengths(jax.random.fold_in(key_of[6], 71), 0)
    cand_feats = scatter_about(key_of[3], (USERS, CANDS, D), 1.0, 6.0, ((0, 16), (1, 16)))
    w_in = scatter_about(key_of[4], (LAYERS, D, 4 * D), D ** -0.5, 0.1875, ((2, 16),))
    w_out = scatter_about(key_of[5], (LAYERS, D, D), D ** -0.5, 0.1875, ((2, 16),))
    return {"kv_cache": kv_cache, "requests": requests, "lengths": lengths, "cand_feats": cand_feats, "w_in": w_in, "w_out": w_out}


def layer_norm(values):
    mean = lax.optimization_barrier(jnp.mean(values, axis=-1, keepdims=True))
    centred = values - mean
    spread = lax.optimization_barrier(jnp.mean(centred * centred, axis=-1, keepdims=True))
    return centred * lax.rsqrt(spread + 1e-06)

def hstu_layer(state, cache, length, w_layer_in, w_layer_out):
    rows = state.shape[0]
    scale = HEAD ** (-0.5)
    normed = layer_norm(state).astype(jnp.bfloat16)
    mixed = jax.nn.silu(jnp.dot(normed, w_layer_in, preferred_element_type=jnp.float32))
    gate = mixed[:, :D]
    value = mixed[:, D:2 * D].astype(jnp.bfloat16).reshape(rows, HEADS, HEAD).astype(jnp.float32)
    query = mixed[:, 2 * D:3 * D].astype(jnp.bfloat16).reshape(rows, HEADS, HEAD).astype(jnp.float32)
    own_key = mixed[:, 3 * D:].astype(jnp.bfloat16).reshape(rows, HEADS, HEAD).astype(jnp.float32)
    past_key = cache[:, :D].reshape(HIST, HEADS, HEAD).astype(jnp.float32)
    past_value = cache[:, D:].reshape(HIST, HEADS, HEAD).astype(jnp.float32)
    scores = jnp.einsum('chd,jhd->hcj', query, past_key) * scale
    live = (jnp.arange(HIST, dtype=jnp.int32) < length).astype(jnp.float32)
    weights = (jax.nn.silu(scores) * live).astype(jnp.bfloat16)
    weights = lax.optimization_barrier(weights).astype(jnp.float32)
    attended = jnp.einsum('hcj,jhd->chd', weights, past_value)
    own = jax.nn.silu(lax.optimization_barrier(jnp.sum(query * own_key, axis=-1)) * scale)
    attended = (attended + own[:, :, None] * value).reshape(rows, D)
    gated = (layer_norm(attended) * gate).astype(jnp.bfloat16)
    return state + jnp.dot(gated, w_layer_out, preferred_element_type=jnp.float32)

def reference(kv_cache, requests, lengths, cand_feats, w_in, w_out):
    owners = N_STORE
    owned = USERS // owners
    per_pair = owned // owners
    table = requests.reshape(owners, owned)
    local = jnp.arange(owned, dtype=jnp.int32)
    same = (table[:, :, None] == table[:, None, :]) & (local[None, None, :] < local[None, :, None])
    rank = lax.optimization_barrier(jnp.sum(same.astype(jnp.int32), axis=2))
    target = table * per_pair + rank
    inverse = lax.optimization_barrier(jnp.sum(jnp.where(target[:, :, None] == local[None, None, :], local[None, :, None], 0), axis=1))
    users = jnp.arange(owners, dtype=jnp.int32)[:, None] * owned + inverse
    slot_user = users.reshape(owners, owners, per_pair).transpose(1, 0, 2).reshape(USERS).astype(jnp.int32)

    def score_slot(slot):
        history = kv_cache[slot_user[slot]]
        state = cand_feats[slot].astype(jnp.float32)
        for layer in range(LAYERS):
            state = hstu_layer(state, history[layer], lengths[slot], w_in[layer], w_out[layer])
        return state.astype(jnp.bfloat16)
    return lax.map(score_slot, jnp.arange(USERS, dtype=jnp.int32))
```

```python
import functools

import jax
import jax.numpy as jnp
from jax import lax
from jax.experimental import pallas as pl
from jax.experimental.pallas import tpu as pltpu
from jax.sharding import PartitionSpec as P

MESH = pl.DeviceIdType.MESH
HEADS = 8
HEAD = 128
SIDE = 4
DEPTH = 8
CORES = 2
F32 = jnp.float32
BF16 = jnp.bfloat16

PLANE = (
    ((1, 0), (3, 0), (0, 1), (0, 3))
    + ((1, 1), (3, 3), (1, 3), (3, 1))
    + ((2, 2), (2, 0), (0, 2))
    + ((2, 1), (2, 3), (1, 2), (3, 2))
)
COLUMN = tuple((dz, dk) for dz in (4, 3, 5, 2, 6, 1, 7) for dk in (0, 1)) + ((0, 1),)


def layer_norm(values):
    mean = jnp.mean(values, axis=-1, keepdims=True)
    centred = values - mean
    spread = jnp.mean(centred * centred, axis=-1, keepdims=True)
    return centred * lax.rsqrt(spread + 1e-06)


def silu_of_double(half):
    return half + half * jnp.tanh(half)


def fold(rows):
    half = rows.shape[1] // 2
    return jnp.concatenate([rows[:, :half], rows[:, half:]], axis=0)


def unfold(piece):
    half = piece.shape[0] // 2
    return jnp.concatenate([piece[:half], piece[half:]], axis=1)


def arrived(region, sem):
    pltpu.make_async_copy(region, region, sem).wait()


def kernel(
    requests,
    lengths,
    kv_hbm,
    feats,
    win_hbm,
    wout_hbm,
    out,
    win,
    wout,
    kv,
    state,
    normed,
    gate,
    mixed,
    attended,
    len_out,
    len_in,
    feat_out,
    feat_in,
    feat_mid,
    feat_here,
    rank_out,
    rank_mid,
    rank_send,
    rank_in,
    inverse,
    send,
    recv,
    z_send,
    z_recv,
    twin_send,
    twin_recv,
):
    me_s = lax.axis_index("store")
    me_c = lax.axis_index("cand")
    z, core = me_s // CORES, lax.rem(me_s, CORES)
    x, y = me_c // SIDE, lax.rem(me_c, SIDE)
    layers, history, _ = kv.shape
    cands, width = state.shape
    users = kv_hbm.shape[0]
    part = cands // users
    rows = history // users
    wide = win.shape[3]
    narrow = wout_hbm.shape[1]

    plane = [
        lax.rem(x + dx, SIDE) * SIDE + lax.rem(y + dy, SIDE) for dx, dy in PLANE
    ]
    column = [
        lax.rem(z + dz, DEPTH) * CORES + lax.rem(core + dk, CORES) for dz, dk in COLUMN
    ]
    barrier = pltpu.get_barrier_semaphore()
    for c in plane:
        pl.semaphore_signal(barrier, inc=1, device_id=(me_s, c), device_id_type=MESH)
    for s in column:
        pl.semaphore_signal(barrier, inc=1, device_id=(s, me_c), device_id_type=MESH)
    for o in range(users):
        len_out[o] = jnp.full((8, 128), lengths[o], jnp.int32)
    for m in range(users // 2):
        both = feats[2 * part * m : 2 * part * (m + 1), :].astype(F32)
        for i in range(2):
            feat_out[2 * m + i] = fold(both[part * i : part * (i + 1)]).astype(BF16)
    pl.semaphore_wait(barrier, len(plane) + len(column))

    def post(src, dst, device, send_sem, recv_sem):
        pltpu.make_async_remote_copy(
            src, dst, send_sem, recv_sem, device_id=device, device_id_type=MESH
        ).start()

    def here(src, dst, sem):
        pltpu.make_async_copy(src, dst, sem).start()

    FEAT_Z, LEN_Z, FEAT_P, RANK_P, RANK_Z, IN0, WO, IN1, KV0, KV1 = range(10)

    depth = width // SIDE // CORES
    quarter = lax.rem(z, SIDE)

    def span(q, k):
        return pl.ds(pl.multiple_of((q * CORES + k) * depth, depth), depth)

    mine = span(quarter, core)
    cols_here = pl.ds(pl.multiple_of(me_c * narrow, narrow), narrow)
    rows_here = pl.ds(pl.multiple_of(me_c * rows, rows), rows)

    for s in column:
        post(feat_out.at[s], feat_in.at[me_s], (s, me_c), send.at[FEAT_Z], recv.at[FEAT_Z])
    here(feat_out.at[me_s], feat_in.at[me_s], recv.at[FEAT_Z])
    for s in column:
        post(len_out.at[s], len_in.at[me_s], (s, me_c), send.at[LEN_Z], recv.at[LEN_Z])
    here(len_out.at[me_s], len_in.at[me_s], recv.at[LEN_Z])

    def spread_in(layer, number):
        src, dst = win_hbm.at[layer, mine], win.at[layer, me_c, mine]
        for c in plane:
            post(src, dst, (me_s, c), send.at[number], recv.at[number])
        here(src, dst, recv.at[number])

    def spread_out():
        src, dst = wout_hbm.at[:, :, mine], wout.at[:, cols_here, mine]
        for c in plane:
            post(src, dst, (me_s, c), send.at[WO], recv.at[WO])
        here(src, dst, recv.at[WO])

    def histories(layer, number):
        dst = kv.at[layer, rows_here]
        for c in plane:
            post(kv_hbm.at[c, layer], dst, (me_s, c), send.at[number], recv.at[number])
        here(kv_hbm.at[me_c, layer], dst, recv.at[number])

    spread_in(0, IN0)
    spread_out()
    spread_in(1, IN1)
    histories(0, KV0)

    arrived(feat_in, recv.at[FEAT_Z])
    for k in range(users):
        feat_mid[k] = feat_in[requests[k]]
    for c in plane:
        post(feat_mid.at[c], feat_here.at[me_c], (me_s, c), send.at[FEAT_P], recv.at[FEAT_P])
    here(feat_mid.at[me_c], feat_here.at[me_c], recv.at[FEAT_P])

    half = users // 2
    up1, down1 = lax.rem(z + 1, DEPTH), lax.rem(z + DEPTH - 1, DEPTH)
    up2, down2 = lax.rem(z + 2, DEPTH), lax.rem(z + DEPTH - 2, DEPTH)

    def in_block(layer, q, k, part_of):
        if part_of is None:
            return win.at[layer, :, span(q, k)]
        return win.at[layer, pl.ds(part_of * half, half), span(q, k)]

    def out_block(_, q, k, part_of):
        if part_of is None:
            return wout.at[:, :, span(q, k)]
        return wout.at[:, pl.ds(part_of * (width // 2), width // 2), span(q, k)]

    def along_z(block, layer, group):
        for i, (to, part_of) in enumerate(
            ((up1, None), (down1, None), (up2, 0), (down2, 1))
        ):
            ref = block(layer, quarter, core, part_of)
            post(ref, ref, (to * CORES + core, me_c), z_send.at[group, i], z_recv.at[group, i])
        to_twin(block(layer, quarter, core, None), group, 0)

    def to_twin(ref, group, i):
        post(ref, ref, (z * CORES + 1 - core, me_c), twin_send.at[group, i], twin_recv.at[group, i])

    def z_blocks(block, layer):
        return [
            block(layer, lax.rem(quarter + step, SIDE), core, part_of)
            for step, part_of in ((3, None), (1, None), (2, 0), (2, 1))
        ]

    def pass_on(block, layer, group):
        for i, ref in enumerate(z_blocks(block, layer)):
            arrived(ref, z_recv.at[group, i])
            to_twin(ref, group, i + 1)

    def from_twin(block, layer, group):
        other = 1 - core
        refs = [block(layer, quarter, other, None)] + [
            block(layer, lax.rem(quarter + step, SIDE), other, part_of)
            for step, part_of in ((3, None), (1, None), (2, 0), (2, 1))
        ]
        for i, ref in enumerate(refs):
            arrived(ref, twin_recv.at[group, i])

    def sent(block, layer, group):
        for i, part_of in enumerate((None, None, 0, 1)):
            arrived(block(layer, quarter, core, part_of), z_send.at[group, i])
        for i, part_of in enumerate((None, None, None, 0, 1)):
            arrived(block(layer, quarter, core, part_of), twin_send.at[group, i])

    arrived(win.at[0, :, mine], recv.at[IN0])
    along_z(in_block, 0, 0)
    arrived(wout.at[:, :, mine], recv.at[WO])
    along_z(out_block, 0, 1)

    for s in range(users):
        at = 0
        for k in range(users):
            at = jnp.where(requests[k] == s, k, at)
        inverse[s] = at

    arrived(feat_here, recv.at[FEAT_P])
    histories(1, KV1)
    for j in range(users):
        state[part * j : part * (j + 1), :] = unfold(feat_here[j].astype(F32))

    block_rows = 32

    def norm_state():
        def step(i, _):
            at = pl.ds(pl.multiple_of(i * block_rows, block_rows), block_rows)
            normed[at, :] = layer_norm(state[at, :]).astype(BF16)
            return 0

        lax.fori_loop(0, cands // block_rows, step, 0)

    def project(layer):
        blocks = width // wide

        def gates(j, _):
            acc = jnp.dot(normed[...], win[layer, j], preferred_element_type=F32)
            at = pl.ds(pl.multiple_of(j * wide, wide), wide)
            gate[:, at] = silu_of_double(0.5 * acc)
            return 0

        lax.fori_loop(0, blocks, gates, 0)

        def others(j, _):
            acc = jnp.dot(normed[...], win[layer, j + blocks], preferred_element_type=F32)
            mixed[j] = silu_of_double(0.5 * acc).astype(BF16)
            return 0

        lax.fori_loop(0, 3 * blocks, others, 0)

    scale = HEAD ** (-0.5)
    pairs = width // wide
    tall = 128

    def attend(layer, live):
        def pair(p, _):
            for i in range(wide // HEAD):
                lanes = slice(i * HEAD, (i + 1) * HEAD)
                at = pl.ds(pl.multiple_of(p * wide + i * HEAD, HEAD), HEAD)
                at_value = pl.ds(pl.multiple_of(width + p * wide + i * HEAD, HEAD), HEAD)
                past_key = kv[layer, :, at]
                past_value = kv[layer, :, at_value]
                for t in range(cands // tall):
                    these = slice(t * tall, (t + 1) * tall)
                    value = mixed[p, these, lanes]
                    query = mixed[p + pairs, these, lanes]
                    own_key = mixed[p + 2 * pairs, these, lanes]
                    scores = lax.dot_general(
                        query, past_key, (((1,), (1,)), ((), ())), preferred_element_type=F32
                    )
                    weights = silu_of_double(scores * live).astype(BF16)
                    total = jnp.dot(weights, past_value, preferred_element_type=F32)
                    own = jnp.sum(
                        query.astype(F32) * own_key.astype(F32), axis=-1, keepdims=True
                    )
                    own = silu_of_double(own * (0.5 * scale))
                    attended[these, at] = total + own * value.astype(F32)
            return 0

        lax.fori_loop(0, pairs, pair, 0)

    def gate_and_add(layer):
        def step(i, _):
            at = pl.ds(pl.multiple_of(i * block_rows, block_rows), block_rows)
            normed[at, :] = (layer_norm(attended[at, :]) * gate[at, :]).astype(BF16)
            return 0

        lax.fori_loop(0, cands // block_rows, step, 0)

        def add(n, _):
            at = pl.ds(pl.multiple_of(n * wide, wide), wide)
            state[:, at] += lax.dot_general(
                normed[...], wout[layer, at, :], (((1,), (1,)), ((), ())), preferred_element_type=F32
            )
            return 0

        lax.fori_loop(0, width // wide, add, 0)

    norm_state()
    arrived(len_in, recv.at[LEN_Z])
    length = len_in[requests[me_c]][:1, :1]
    position = lax.broadcasted_iota(jnp.int32, (1, history), 1)
    live = jnp.where(position < length, 0.5 * scale, 0.0).astype(F32)

    pass_on(in_block, 0, 0)
    pass_on(out_block, 0, 1)
    arrived(win.at[1, :, mine], recv.at[IN1])
    along_z(in_block, 1, 2)
    from_twin(in_block, 0, 0)
    project(0)
    arrived(kv.at[0], recv.at[KV0])
    attend(0, live)
    from_twin(out_block, 0, 1)
    gate_and_add(0)

    norm_state()
    pass_on(in_block, 1, 2)
    from_twin(in_block, 1, 2)
    project(1)
    arrived(kv.at[1], recv.at[KV1])
    attend(1, live)
    gate_and_add(1)

    for j in range(users):
        rank_out[j] = fold(state[part * j : part * (j + 1), :]).astype(BF16)
    for c in plane:
        post(rank_out.at[c], rank_mid.at[me_c], (me_s, c), send.at[RANK_P], recv.at[RANK_P])
    here(rank_out.at[me_c], rank_mid.at[me_c], recv.at[RANK_P])
    arrived(rank_mid, recv.at[RANK_P])
    for s in range(users):
        rank_send[s] = rank_mid[inverse[s]]
    for s in column:
        post(rank_send.at[s], rank_in.at[me_s], (s, me_c), send.at[RANK_Z], recv.at[RANK_Z])
    here(rank_send.at[me_s], rank_in.at[me_s], recv.at[RANK_Z])
    arrived(rank_in, recv.at[RANK_Z])
    for m in range(users // 2):
        both = [unfold(rank_in[2 * m + i].astype(F32)) for i in range(2)]
        out[2 * part * m : 2 * part * (m + 1), :] = jnp.concatenate(both, axis=0).astype(BF16)

    others = pl.ds(0, users - 1)
    arrived(feat_out.at[others], send.at[FEAT_Z])
    arrived(len_out.at[others], send.at[LEN_Z])
    arrived(feat_mid.at[others], send.at[FEAT_P])
    arrived(rank_out.at[others], send.at[RANK_P])
    arrived(rank_send.at[others], send.at[RANK_Z])
    arrived(win.at[0, others, mine], send.at[IN0])
    arrived(win.at[1, others, mine], send.at[IN1])
    arrived(wout.at[:, pl.ds(0, (users - 1) * narrow), mine], send.at[WO])
    arrived(kv.at[0, pl.ds(0, (users - 1) * rows)], send.at[KV0])
    arrived(kv.at[1, pl.ds(0, (users - 1) * rows)], send.at[KV1])
    sent(in_block, 0, 0)
    sent(out_block, 0, 1)
    sent(in_block, 1, 2)


def shards(kv_cache, requests, lengths, cand_feats, w_in, w_out):
    users, layers, rows, _ = kv_cache.shape
    _, part, width = cand_feats.shape
    cands, history = users * part, users * rows
    wide = w_in.shape[2]
    vmem = pl.BlockSpec(memory_space=pltpu.VMEM)
    smem = pl.BlockSpec(memory_space=pltpu.SMEM)
    anywhere = pl.BlockSpec(memory_space=pl.ANY)
    piece = pltpu.VMEM((users, 2 * part, width // 2), BF16)
    flops = layers * (2 * cands * width * 5 * width + 4 * cands * history * width)
    ranked = pl.pallas_call(
        kernel,
        out_shape=jax.ShapeDtypeStruct((cands, width), BF16),
        in_specs=[smem, smem, anywhere, vmem, anywhere, anywhere],
        out_specs=vmem,
        scratch_shapes=[
            pltpu.VMEM((layers, users, width, wide), BF16),
            pltpu.VMEM((layers, width, width), BF16),
            pltpu.VMEM((layers, history, 2 * width), BF16),
            pltpu.VMEM((cands, width), F32),
            pltpu.VMEM((cands, width), BF16),
            pltpu.VMEM((cands, width), F32),
            pltpu.VMEM((3 * width // wide, cands, wide), BF16),
            pltpu.VMEM((cands, width), F32),
            pltpu.VMEM((users, 8, 128), jnp.int32),
            pltpu.VMEM((users, 8, 128), jnp.int32),
            *[piece] * 8,
            pltpu.SMEM((users,), jnp.int32),
            pltpu.SemaphoreType.DMA((10,)),
            pltpu.SemaphoreType.DMA((10,)),
            pltpu.SemaphoreType.DMA((3, 4)),
            pltpu.SemaphoreType.DMA((3, 4)),
            pltpu.SemaphoreType.DMA((3, 5)),
            pltpu.SemaphoreType.DMA((3, 5)),
        ],
        compiler_params=pltpu.CompilerParams(
            collective_id=0, has_side_effects=True, vmem_limit_bytes=60 * 1024 * 1024
        ),
        cost_estimate=pl.CostEstimate(
            flops=flops, bytes_accessed=64 * 1024 * 1024, transcendentals=cands * width * 24
        ),
        name="rank_two_layers",
    )(requests, lengths, kv_cache, cand_feats.reshape(cands, width), w_in, jnp.swapaxes(w_out, 1, 2))
    return ranked.reshape(cand_feats.shape)


def solution(mesh):
    return jax.shard_map(
        shards,
        mesh=mesh,
        in_specs=(
            P("store", None, "cand", None),
            P("store"),
            P("store"),
            P("store", "cand", None),
            P(None, None, "cand"),
            P(None, None, "cand"),
        ),
        out_specs=P("store", "cand", None),
        check_vma=False,
    )
```

```python
import functools

import jax
import jax.numpy as jnp
from jax import lax
from jax.experimental import pallas as pl
from jax.experimental.pallas import tpu as pltpu
from jax.sharding import PartitionSpec as P

MESH = pl.DeviceIdType.MESH
HEADS = 8
HEAD = 128
SIDE = 4
DEPTH = 8
LOW = 8
CORES = 2
F32 = jnp.float32
BF16 = jnp.bfloat16

PLANE = (
    ((1, 0), (3, 0), (0, 1), (0, 3))
    + ((1, 1), (3, 3), (1, 3), (3, 1))
    + ((2, 2), (2, 0), (0, 2))
    + ((2, 1), (2, 3), (1, 2), (3, 2))
)
COLUMN = tuple((dz, dk) for dz in (4, 3, 5, 2, 6, 1, 7) for dk in (0, 1)) + ((0, 1),)


def layer_norm(values):
    mean = jnp.mean(values, axis=-1, keepdims=True)
    centred = values - mean
    spread = jnp.mean(centred * centred, axis=-1, keepdims=True)
    return centred * lax.rsqrt(spread + 1e-06)


def silu_of_double(half):
    return half + half * jnp.tanh(half)


def fold(rows):
    half = rows.shape[1] // 2
    return jnp.concatenate([rows[:, :half], rows[:, half:]], axis=0)


def unfold(piece):
    half = piece.shape[0] // 2
    return jnp.concatenate([piece[:half], piece[half:]], axis=1)


def arrived(region, sem):
    pltpu.make_async_copy(region, region, sem).wait()


def kernel(
    requests,
    lengths,
    kv_hbm,
    feats,
    win_hbm,
    wout_hbm,
    out,
    win,
    wout,
    kv,
    state,
    normed,
    gate,
    mixed,
    attended,
    len_out,
    len_in,
    feat_out,
    feat_in,
    feat_mid,
    feat_here,
    rank_out,
    rank_send,
    rank_in,
    inverse,
    send,
    recv,
    a_send,
    a_recv,
    b_send,
    b_recv,
    z_send,
    z_recv,
    twin_send,
    twin_recv,
    *rank_mid,
):
    me_s = lax.axis_index("store")
    me_c = lax.axis_index("cand")
    z, core = me_s // CORES, lax.rem(me_s, CORES)
    x, y = me_c // SIDE, lax.rem(me_c, SIDE)
    layers, history, _ = kv.shape
    cands, width = state.shape
    users = kv_hbm.shape[0]
    part = cands // users
    tiles = part // LOW
    tall = users * LOW
    rows = history // users
    wide = win.shape[4]
    narrow = wout_hbm.shape[1]

    plane = [
        lax.rem(x + dx, SIDE) * SIDE + lax.rem(y + dy, SIDE) for dx, dy in PLANE
    ]
    column = [
        lax.rem(z + dz, DEPTH) * CORES + lax.rem(core + dk, CORES) for dz, dk in COLUMN
    ]
    barrier = pltpu.get_barrier_semaphore()
    for c in plane:
        pl.semaphore_signal(barrier, inc=1, device_id=(me_s, c), device_id_type=MESH)
    for s in column:
        pl.semaphore_signal(barrier, inc=1, device_id=(s, me_c), device_id_type=MESH)
    for o in range(users):
        len_out[o] = jnp.full((8, 128), lengths[o], jnp.int32)
    pl.semaphore_wait(barrier, len(plane) + len(column))

    def post(src, dst, device, send_sem, recv_sem):
        pltpu.make_async_remote_copy(
            src, dst, send_sem, recv_sem, device_id=device, device_id_type=MESH
        ).start()

    def here(src, dst, sem):
        pltpu.make_async_copy(src, dst, sem).start()

    FEAT_Z, LEN_Z, FEAT_P, KV0, KEY1, VALUE1, KEY1_LAST, VALUE1_LAST, RANK_P = range(9)
    RANK_Z = RANK_P + tiles
    early = width - wide
    IN0, WO, IN1 = range(3)

    depth = width // SIDE // CORES
    quarter = lax.rem(z, SIDE)

    def span(q, k, start=0, size=depth):
        return pl.ds(pl.multiple_of((q * CORES + k) * depth + start, size), size)

    rows_here = pl.ds(pl.multiple_of(me_c * rows, rows), rows)
    steps = (1, 3, 2)
    x_peers = [lax.rem(x + d, SIDE) * SIDE + y for d in steps]
    y_peers = [x * SIDE + lax.rem(y + d, SIDE) for d in steps]
    x_from = [lax.rem(x + SIDE - d, SIDE) for d in steps]
    y_from = [lax.rem(y + SIDE - d, SIDE) for d in steps]
    every = slice(None)

    def share(group, axis, at_x, at_y):
        if group == WO:
            low = narrow // 2
            return wout.at[:, at_x, at_y, pl.ds(axis * low, low), span(quarter, core)]
        low = depth // 2
        return win.at[group // 2, at_x, at_y, span(quarter, core, axis * low, low)]

    def source(group, axis):
        if group == WO:
            low = narrow // 2
            return wout_hbm.at[:, pl.ds(axis * low, low), span(quarter, core)]
        low = depth // 2
        return win_hbm.at[group // 2, span(quarter, core, axis * low, low)]

    def line(group, axis):
        return share(group, axis, every, y) if axis == 0 else share(group, axis, x, every)

    def spread_first(group):
        for axis, peers in enumerate((x_peers, y_peers)):
            src, dst = source(group, axis), share(group, axis, x, y)
            for c in peers:
                post(src, dst, (me_s, c), a_send.at[group, axis], a_recv.at[group, axis])
            here(src, dst, a_recv.at[group, axis])

    def spread_second(group):
        for axis, peers in enumerate((y_peers, x_peers)):
            ref = line(group, axis)
            arrived(ref, a_recv.at[group, axis])
            for i, c in enumerate(peers):
                post(ref, ref, (me_s, c), b_send.at[group, axis, i], b_recv.at[group, axis, i])

    def spread_end(group):
        for i in range(len(steps)):
            arrived(share(group, 0, every, y_from[i]), b_recv.at[group, 0, i])
            arrived(share(group, 1, x_from[i], every), b_recv.at[group, 1, i])

    def spread_sent(group):
        most = pl.ds(0, SIDE - 1)
        arrived(share(group, 0, most, y), a_send.at[group, 0])
        arrived(share(group, 1, x, most), a_send.at[group, 1])
        for i in range(len(steps)):
            arrived(line(group, 0), b_send.at[group, 0, i])
            arrived(line(group, 1), b_send.at[group, 1, i])

    def histories(layer, number, first, size):
        lanes = pl.ds(first, size)
        dst = kv.at[layer, rows_here, lanes]
        for c in plane:
            src = kv_hbm.at[c, layer, :, lanes]
            post(src, dst, (me_s, c), send.at[number], recv.at[number])
        here(kv_hbm.at[me_c, layer, :, lanes], dst, recv.at[number])

    def histories_sent(layer, number, first, size):
        lanes = pl.ds(first, size)
        arrived(kv.at[layer, pl.ds(0, (users - 1) * rows), lanes], send.at[number])

    up, down = lax.rem(z + 1, DEPTH) * CORES, lax.rem(z + DEPTH - 1, DEPTH) * CORES
    twin = z * CORES + 1 - core
    ahead, behind, across = (lax.rem(quarter + d, SIDE) for d in (1, 3, 2))
    low, high = pl.ds(0, SIDE // 2), pl.ds(SIDE // 2, SIDE // 2)

    def block(group, q, k, part_of=every):
        if group == WO:
            return wout.at[:, part_of, :, :, span(q, k)]
        return win.at[group // 2, part_of, :, span(q, k)]

    def along(ref, to, group, i):
        post(ref, ref, (to + core, me_c), z_send.at[group, i], z_recv.at[group, i])

    def to_twin(ref, group, i):
        post(ref, ref, (twin, me_c), twin_send.at[group, i], twin_recv.at[group, i])

    def z_first(group):
        ref = block(group, quarter, core)
        along(ref, up, group, 0)
        along(ref, down, group, 1)
        to_twin(ref, group, 0)

    def z_second(group):
        for i, (q, to, part_of) in enumerate(((behind, up, low), (ahead, down, high))):
            arrived(block(group, q, core), z_recv.at[group, i])
            along(block(group, q, core, part_of), to, group, 2 + i)
            to_twin(block(group, q, core), group, 1 + i)

    def z_end(group):
        for i, part_of in enumerate((low, high)):
            ref = block(group, across, core, part_of)
            arrived(ref, z_recv.at[group, 2 + i])
            to_twin(ref, group, 3 + i)

    def from_twin(group):
        for i, (q, part_of) in enumerate(
            ((quarter, every), (behind, every), (ahead, every), (across, low), (across, high))
        ):
            arrived(block(group, q, 1 - core, part_of), twin_recv.at[group, i])

    def z_sent(group):
        whole, part_of = block(group, quarter, core), block(group, quarter, core, low)
        for i in range(4):
            arrived(whole if i < 2 else part_of, z_send.at[group, i])
        for i in range(5):
            arrived(whole if i < 3 else part_of, twin_send.at[group, i])

    spread_first(IN0)
    spread_first(WO)

    for m in range(users // 2):
        both = feats[2 * part * m : 2 * part * (m + 1), :].astype(F32)
        for i in range(2):
            for t in range(tiles):
                first = part * i + LOW * t
                feat_out[2 * m + i, 2 * LOW * t : 2 * LOW * (t + 1), :] = fold(
                    both[first : first + LOW]
                ).astype(BF16)
    for s in column:
        post(feat_out.at[s], feat_in.at[me_s], (s, me_c), send.at[FEAT_Z], recv.at[FEAT_Z])
    here(feat_out.at[me_s], feat_in.at[me_s], recv.at[FEAT_Z])
    for s in column:
        post(len_out.at[s], len_in.at[me_s], (s, me_c), send.at[LEN_Z], recv.at[LEN_Z])
    here(len_out.at[me_s], len_in.at[me_s], recv.at[LEN_Z])

    spread_second(IN0)
    spread_first(IN1)
    spread_second(WO)
    spread_end(IN0)
    z_first(IN0)
    spread_second(IN1)
    histories(0, KV0, 0, 2 * width)
    spread_end(WO)
    z_first(WO)
    spread_end(IN1)

    arrived(feat_in, recv.at[FEAT_Z])
    for k in range(users):
        feat_mid[k] = feat_in[requests[k]]
    for c in plane:
        post(feat_mid.at[c], feat_here.at[me_c], (me_s, c), send.at[FEAT_P], recv.at[FEAT_P])
    here(feat_mid.at[me_c], feat_here.at[me_c], recv.at[FEAT_P])

    for s in range(users):
        at = 0
        for k in range(users):
            at = jnp.where(requests[k] == s, k, at)
        inverse[s] = at

    arrived(feat_here, recv.at[FEAT_P])
    for j in range(users):
        for t in range(tiles):
            state[tall * t + LOW * j : tall * t + LOW * (j + 1), :] = unfold(
                feat_here[j, 2 * LOW * t : 2 * LOW * (t + 1), :].astype(F32)
            )

    block_rows = 32

    def norm_state():
        def step(i, _):
            at = pl.ds(pl.multiple_of(i * block_rows, block_rows), block_rows)
            normed[at, :] = layer_norm(state[at, :]).astype(BF16)
            return 0

        lax.fori_loop(0, cands // block_rows, step, 0)

    def project(layer):
        blocks = width // wide

        def gates(j, _):
            acc = jnp.dot(normed[...], win[layer, 0, j], preferred_element_type=F32)
            at = pl.ds(pl.multiple_of(j * wide, wide), wide)
            gate[:, at] = silu_of_double(0.5 * acc)
            return 0

        lax.fori_loop(0, blocks, gates, 0)

        def others(j, _):
            acc = jnp.dot(normed[...], win[layer, 1 + j // SIDE, lax.rem(j, SIDE)], preferred_element_type=F32)
            mixed[j] = silu_of_double(0.5 * acc).astype(BF16)
            return 0

        lax.fori_loop(0, 3 * blocks, others, 0)

    scale = HEAD ** (-0.5)
    pairs = width // wide

    def attend_pair(layer, p, which):
        for i in range(wide // HEAD):
            lanes = slice(i * HEAD, (i + 1) * HEAD)
            at = pl.ds(pl.multiple_of(p * wide + i * HEAD, HEAD), HEAD)
            at_value = pl.ds(pl.multiple_of(width + p * wide + i * HEAD, HEAD), HEAD)
            past_key = kv[layer, :, at]
            past_value = kv[layer, :, at_value]
            for t in which:
                these = slice(t * tall, (t + 1) * tall)
                value = mixed[p, these, lanes]
                query = mixed[p + pairs, these, lanes]
                own_key = mixed[p + 2 * pairs, these, lanes]
                scores = lax.dot_general(
                    query, past_key, (((1,), (1,)), ((), ())), preferred_element_type=F32
                )
                weights = silu_of_double(scores * live).astype(BF16)
                total = jnp.dot(weights, past_value, preferred_element_type=F32)
                own = jnp.sum(query.astype(F32) * own_key.astype(F32), axis=-1, keepdims=True)
                own = silu_of_double(own * (0.5 * scale))
                attended[these, at] = total + own * value.astype(F32)

    def attend(layer, count):
        def step(p, _):
            attend_pair(layer, p, range(tiles))
            return 0

        lax.fori_loop(0, count, step, 0)

    def gate_and_add(layer, first, size):
        def step(i, _):
            at = pl.ds(pl.multiple_of(first + i * block_rows, block_rows), block_rows)
            normed[at, :] = (layer_norm(attended[at, :]) * gate[at, :]).astype(BF16)
            return 0

        lax.fori_loop(0, size // block_rows, step, 0)
        these = slice(first, first + size)

        def add(n, _):
            at = pl.ds(pl.multiple_of(n * wide, wide), wide)
            columns = wout[layer, n].reshape(wide, width)
            state[these, at] += lax.dot_general(
                normed[these, :], columns, (((1,), (1,)), ((), ())), preferred_element_type=F32
            )
            return 0

        lax.fori_loop(0, width // wide, add, 0)

    norm_state()
    arrived(len_in, recv.at[LEN_Z])
    length = len_in[requests[me_c]][:1, :1]
    position = lax.broadcasted_iota(jnp.int32, (1, history), 1)
    live = jnp.where(position < length, 0.5 * scale, 0.0).astype(F32)

    histories(1, KEY1, 0, early)
    histories(1, VALUE1, width, early)
    histories(1, KEY1_LAST, early, wide)
    histories(1, VALUE1_LAST, width + early, wide)

    z_second(IN0)
    z_second(WO)
    z_end(IN0)
    z_first(IN1)
    from_twin(IN0)
    project(0)
    z_end(WO)
    arrived(kv.at[0], recv.at[KV0])
    attend(0, pairs)
    from_twin(WO)
    gate_and_add(0, 0, cands)

    z_second(IN1)
    norm_state()
    z_end(IN1)
    from_twin(IN1)
    project(1)
    arrived(kv.at[1, :, pl.ds(0, early)], recv.at[KEY1])
    arrived(kv.at[1, :, pl.ds(width, early)], recv.at[VALUE1])
    attend(1, pairs - 1)
    arrived(kv.at[1, :, pl.ds(early, wide)], recv.at[KEY1_LAST])
    arrived(kv.at[1, :, pl.ds(width + early, wide)], recv.at[VALUE1_LAST])

    def back(t):
        for j in range(users):
            rank_out[t, j] = fold(state[tall * t + LOW * j : tall * t + LOW * (j + 1), :]).astype(BF16)
        for c in plane:
            post(rank_out.at[t, c], rank_mid[t].at[me_c], (me_s, c), send.at[RANK_P + t], recv.at[RANK_P + t])
        here(rank_out.at[t, me_c], rank_mid[t].at[me_c], recv.at[RANK_P + t])

    def home(t):
        arrived(rank_mid[t], recv.at[RANK_P + t])
        for s in range(users):
            rank_send[t, s] = rank_mid[t][inverse[s]]
        for s in column:
            post(rank_send.at[t, s], rank_in.at[t, me_s], (s, me_c), send.at[RANK_Z + t], recv.at[RANK_Z + t])
        here(rank_send.at[t, me_s], rank_in.at[t, me_s], recv.at[RANK_Z + t])

    for t in range(tiles):
        attend_pair(1, pairs - 1, (t,))
        gate_and_add(1, t * tall, tall)
        back(t)
        if t > 0:
            home(t - 1)
    home(tiles - 1)
    for t in range(tiles):
        arrived(rank_in.at[t], recv.at[RANK_Z + t])
    for m in range(users // 2):
        both = [
            unfold(rank_in[t, 2 * m + i].astype(F32)) for i in range(2) for t in range(tiles)
        ]
        out[2 * part * m : 2 * part * (m + 1), :] = jnp.concatenate(both, axis=0).astype(BF16)

    others = pl.ds(0, users - 1)
    arrived(feat_out.at[others], send.at[FEAT_Z])
    arrived(len_out.at[others], send.at[LEN_Z])
    arrived(feat_mid.at[others], send.at[FEAT_P])
    for t in range(tiles):
        arrived(rank_out.at[t, others], send.at[RANK_P + t])
        arrived(rank_send.at[t, others], send.at[RANK_Z + t])
    histories_sent(0, KV0, 0, 2 * width)
    histories_sent(1, KEY1, 0, early)
    histories_sent(1, VALUE1, width, early)
    histories_sent(1, KEY1_LAST, early, wide)
    histories_sent(1, VALUE1_LAST, width + early, wide)
    for group in (IN0, WO, IN1):
        spread_sent(group)
        z_sent(group)


def shards(kv_cache, requests, lengths, cand_feats, w_in, w_out):
    users, layers, rows, _ = kv_cache.shape
    _, part, width = cand_feats.shape
    cands, history = users * part, users * rows
    wide = w_in.shape[2]
    vmem = pl.BlockSpec(memory_space=pltpu.VMEM)
    smem = pl.BlockSpec(memory_space=pltpu.SMEM)
    anywhere = pl.BlockSpec(memory_space=pl.ANY)
    piece = pltpu.VMEM((users, 2 * part, width // 2), BF16)
    tiles = part // LOW
    tile = pltpu.VMEM((tiles, users, 2 * LOW, width // 2), BF16)
    flops = layers * (2 * cands * width * 5 * width + 4 * cands * history * width)
    ranked = pl.pallas_call(
        kernel,
        out_shape=jax.ShapeDtypeStruct((cands, width), BF16),
        in_specs=[smem, smem, anywhere, vmem, anywhere, anywhere],
        out_specs=vmem,
        scratch_shapes=[
            pltpu.VMEM((layers, SIDE, SIDE, width, wide), BF16),
            pltpu.VMEM((layers, SIDE, SIDE, width // users, width), BF16),
            pltpu.VMEM((layers, history, 2 * width), BF16),
            pltpu.VMEM((cands, width), F32),
            pltpu.VMEM((cands, width), BF16),
            pltpu.VMEM((cands, width), F32),
            pltpu.VMEM((3 * width // wide, cands, wide), BF16),
            pltpu.VMEM((cands, width), F32),
            pltpu.VMEM((users, 8, 128), jnp.int32),
            pltpu.VMEM((users, 8, 128), jnp.int32),
            *[piece] * 4,
            *[tile] * 3,
            pltpu.SMEM((users,), jnp.int32),
            pltpu.SemaphoreType.DMA((9 + 2 * tiles,)),
            pltpu.SemaphoreType.DMA((9 + 2 * tiles,)),
            pltpu.SemaphoreType.DMA((3, 2)),
            pltpu.SemaphoreType.DMA((3, 2)),
            pltpu.SemaphoreType.DMA((3, 2, 3)),
            pltpu.SemaphoreType.DMA((3, 2, 3)),
            pltpu.SemaphoreType.DMA((3, 4)),
            pltpu.SemaphoreType.DMA((3, 4)),
            pltpu.SemaphoreType.DMA((3, 5)),
            pltpu.SemaphoreType.DMA((3, 5)),
            *[pltpu.VMEM((users, 2 * LOW, width // 2), BF16)] * tiles,
        ],
        compiler_params=pltpu.CompilerParams(
            collective_id=0, has_side_effects=True, vmem_limit_bytes=60 * 1024 * 1024
        ),
        cost_estimate=pl.CostEstimate(
            flops=flops, bytes_accessed=64 * 1024 * 1024, transcendentals=cands * width * 24
        ),
        name="rank_two_layers",
    )(requests, lengths, kv_cache, cand_feats.reshape(cands, width), w_in, jnp.swapaxes(w_out, 1, 2))
    return ranked.reshape(cand_feats.shape)


def solution(mesh):
    return jax.shard_map(
        shards,
        mesh=mesh,
        in_specs=(
            P("store", None, "cand", None),
            P("store"),
            P("store"),
            P("store", "cand", None),
            P(None, None, "cand"),
            P(None, None, "cand"),
        ),
        out_specs=P("store", "cand", None),
        check_vma=False,
    )
```

```python
import functools

import jax
import jax.numpy as jnp
from jax import lax
from jax.experimental import pallas as pl
from jax.experimental.pallas import tpu as pltpu
from jax.sharding import PartitionSpec as P

MESH = pl.DeviceIdType.MESH
HEADS = 8
HEAD = 128
SIDE = 4
DEPTH = 8
LOW = 8
CORES = 2
F32 = jnp.float32
BF16 = jnp.bfloat16

PLANE = (
    ((1, 0), (3, 0), (0, 1), (0, 3))
    + ((1, 1), (3, 3), (1, 3), (3, 1))
    + ((2, 2), (2, 0), (0, 2))
    + ((2, 1), (2, 3), (1, 2), (3, 2))
)
COLUMN = tuple((dz, dk) for dz in (4, 3, 5, 2, 6, 1, 7) for dk in (0, 1)) + ((0, 1),)


def layer_norm(values):
    mean = jnp.mean(values, axis=-1, keepdims=True)
    centred = values - mean
    spread = jnp.mean(centred * centred, axis=-1, keepdims=True)
    return centred * lax.rsqrt(spread + 1e-06)


def silu_of_double(half):
    return half + half * jnp.tanh(half)


def fold(rows):
    half = rows.shape[1] // 2
    return jnp.concatenate([rows[:, :half], rows[:, half:]], axis=0)


def unfold(piece):
    half = piece.shape[0] // 2
    return jnp.concatenate([piece[:half], piece[half:]], axis=1)


def arrived(region, sem):
    pltpu.make_async_copy(region, region, sem).wait()


def kernel(
    requests,
    lengths,
    kv_hbm,
    feats,
    win_hbm,
    wout_hbm,
    out,
    win,
    wout,
    kv,
    state,
    normed,
    gate,
    mixed,
    attended,
    len_out,
    len_in,
    feat_out,
    feat_in,
    feat_mid,
    feat_here,
    rank_out,
    rank_send,
    rank_in,
    inverse,
    send,
    recv,
    a_send,
    a_recv,
    b_send,
    b_recv,
    z_send,
    z_recv,
    twin_send,
    twin_recv,
    *rank_mid,
):
    me_s = lax.axis_index("store")
    me_c = lax.axis_index("cand")
    z, core = me_s // CORES, lax.rem(me_s, CORES)
    x, y = me_c // SIDE, lax.rem(me_c, SIDE)
    layers, history, _ = kv.shape
    cands, width = state.shape
    users = kv_hbm.shape[0]
    part = cands // users
    tiles = part // LOW
    tall = users * LOW
    rows = history // users
    wide = win.shape[4]
    narrow = wout_hbm.shape[1]

    plane = [
        lax.rem(x + dx, SIDE) * SIDE + lax.rem(y + dy, SIDE) for dx, dy in PLANE
    ]
    column = [
        lax.rem(z + dz, DEPTH) * CORES + lax.rem(core + dk, CORES) for dz, dk in COLUMN
    ]
    barrier = pltpu.get_barrier_semaphore()
    for c in plane:
        pl.semaphore_signal(barrier, inc=1, device_id=(me_s, c), device_id_type=MESH)
    for s in column:
        pl.semaphore_signal(barrier, inc=1, device_id=(s, me_c), device_id_type=MESH)
    for o in range(users):
        len_out[o] = jnp.full((8, 128), lengths[o], jnp.int32)
    pl.semaphore_wait(barrier, len(plane) + len(column))

    def post(src, dst, device, send_sem, recv_sem):
        pltpu.make_async_remote_copy(
            src, dst, send_sem, recv_sem, device_id=device, device_id_type=MESH
        ).start()

    def here(src, dst, sem):
        pltpu.make_async_copy(src, dst, sem).start()

    FEAT_Z, LEN_Z, FEAT_P, KV0, KEY1, VALUE1, KEY1_LAST, VALUE1_LAST, RANK_P = range(9)
    RANK_Z = RANK_P + tiles
    early = width - wide
    IN0, WO, IN1 = range(3)

    depth = width // SIDE // CORES
    quarter = lax.rem(z, SIDE)

    def span(q, k, start=0, size=depth):
        return pl.ds(pl.multiple_of((q * CORES + k) * depth + start, size), size)

    rows_here = pl.ds(pl.multiple_of(me_c * rows, rows), rows)
    steps = (1, 3, 2)
    x_peers = [lax.rem(x + d, SIDE) * SIDE + y for d in steps]
    y_peers = [x * SIDE + lax.rem(y + d, SIDE) for d in steps]
    x_from = [lax.rem(x + SIDE - d, SIDE) for d in steps]
    y_from = [lax.rem(y + SIDE - d, SIDE) for d in steps]
    every = slice(None)

    def share(group, axis, at_x, at_y):
        if group == WO:
            low = narrow // 2
            return wout.at[:, at_x, at_y, pl.ds(axis * low, low), span(quarter, core)]
        low = depth // 2
        return win.at[group // 2, at_x, at_y, span(quarter, core, axis * low, low)]

    def source(group, axis):
        if group == WO:
            low = narrow // 2
            return wout_hbm.at[:, pl.ds(axis * low, low), span(quarter, core)]
        low = depth // 2
        return win_hbm.at[group // 2, span(quarter, core, axis * low, low)]

    def line(group, axis):
        return share(group, axis, every, y) if axis == 0 else share(group, axis, x, every)

    def spread_first(group):
        for axis, peers in enumerate((x_peers, y_peers)):
            src, dst = source(group, axis), share(group, axis, x, y)
            for c in peers:
                post(src, dst, (me_s, c), a_send.at[group, axis], a_recv.at[group, axis])
            here(src, dst, a_recv.at[group, axis])

    def spread_second(group):
        for axis, peers in enumerate((y_peers, x_peers)):
            ref = line(group, axis)
            arrived(ref, a_recv.at[group, axis])
            for i, c in enumerate(peers):
                post(ref, ref, (me_s, c), b_send.at[group, axis, i], b_recv.at[group, axis, i])

    def spread_end(group):
        for i in range(len(steps)):
            arrived(share(group, 0, every, y_from[i]), b_recv.at[group, 0, i])
            arrived(share(group, 1, x_from[i], every), b_recv.at[group, 1, i])

    def spread_sent(group):
        most = pl.ds(0, SIDE - 1)
        arrived(share(group, 0, most, y), a_send.at[group, 0])
        arrived(share(group, 1, x, most), a_send.at[group, 1])
        for i in range(len(steps)):
            arrived(line(group, 0), b_send.at[group, 0, i])
            arrived(line(group, 1), b_send.at[group, 1, i])

    def histories(layer, number, first, size):
        lanes = pl.ds(first, size)
        dst = kv.at[layer, rows_here, lanes]
        for c in plane:
            src = kv_hbm.at[c, layer, :, lanes]
            post(src, dst, (me_s, c), send.at[number], recv.at[number])
        here(kv_hbm.at[me_c, layer, :, lanes], dst, recv.at[number])

    def histories_sent(layer, number, first, size):
        lanes = pl.ds(first, size)
        arrived(kv.at[layer, pl.ds(0, (users - 1) * rows), lanes], send.at[number])

    up, down = lax.rem(z + 1, DEPTH) * CORES, lax.rem(z + DEPTH - 1, DEPTH) * CORES
    twin = z * CORES + 1 - core
    ahead, behind, across = (lax.rem(quarter + d, SIDE) for d in (1, 3, 2))
    low, high = pl.ds(0, SIDE // 2), pl.ds(SIDE // 2, SIDE // 2)

    def block(group, q, k, part_of=every):
        if group == WO:
            return wout.at[:, part_of, :, :, span(q, k)]
        return win.at[group // 2, part_of, :, span(q, k)]

    def along(ref, to, group, i):
        post(ref, ref, (to + core, me_c), z_send.at[group, i], z_recv.at[group, i])

    def to_twin(ref, group, i):
        post(ref, ref, (twin, me_c), twin_send.at[group, i], twin_recv.at[group, i])

    def z_first(group):
        ref = block(group, quarter, core)
        along(ref, up, group, 0)
        along(ref, down, group, 1)
        to_twin(ref, group, 0)

    def z_second(group):
        for i, (q, to, part_of) in enumerate(((behind, up, low), (ahead, down, high))):
            arrived(block(group, q, core), z_recv.at[group, i])
            along(block(group, q, core, part_of), to, group, 2 + i)
            to_twin(block(group, q, core), group, 1 + i)

    def z_end(group):
        for i, part_of in enumerate((low, high)):
            ref = block(group, across, core, part_of)
            arrived(ref, z_recv.at[group, 2 + i])
            to_twin(ref, group, 3 + i)

    def from_twin(group):
        for i, (q, part_of) in enumerate(
            ((quarter, every), (behind, every), (ahead, every), (across, low), (across, high))
        ):
            arrived(block(group, q, 1 - core, part_of), twin_recv.at[group, i])

    def z_sent(group):
        whole, part_of = block(group, quarter, core), block(group, quarter, core, low)
        for i in range(4):
            arrived(whole if i < 2 else part_of, z_send.at[group, i])
        for i in range(5):
            arrived(whole if i < 3 else part_of, twin_send.at[group, i])

    spread_first(IN0)
    spread_first(WO)

    for m in range(users // 2):
        both = feats[2 * part * m : 2 * part * (m + 1), :].astype(F32)
        for i in range(2):
            for t in range(tiles):
                first = part * i + LOW * t
                feat_out[2 * m + i, 2 * LOW * t : 2 * LOW * (t + 1), :] = fold(
                    both[first : first + LOW]
                ).astype(BF16)
    for s in column:
        post(feat_out.at[s], feat_in.at[me_s], (s, me_c), send.at[FEAT_Z], recv.at[FEAT_Z])
    here(feat_out.at[me_s], feat_in.at[me_s], recv.at[FEAT_Z])
    for s in column:
        post(len_out.at[s], len_in.at[me_s], (s, me_c), send.at[LEN_Z], recv.at[LEN_Z])
    here(len_out.at[me_s], len_in.at[me_s], recv.at[LEN_Z])

    spread_second(IN0)
    spread_first(IN1)
    spread_second(WO)
    spread_end(IN0)
    z_first(IN0)
    spread_second(IN1)
    spread_end(WO)
    z_first(WO)
    spread_end(IN1)

    histories(0, KV0, 0, 2 * width)
    arrived(feat_in, recv.at[FEAT_Z])
    for k in range(users):
        feat_mid[k] = feat_in[requests[k]]
    for c in plane:
        post(feat_mid.at[c], feat_here.at[me_c], (me_s, c), send.at[FEAT_P], recv.at[FEAT_P])
    here(feat_mid.at[me_c], feat_here.at[me_c], recv.at[FEAT_P])

    for s in range(users):
        at = 0
        for k in range(users):
            at = jnp.where(requests[k] == s, k, at)
        inverse[s] = at

    z_second(IN0)
    z_first(IN1)
    z_second(WO)
    histories(1, KEY1, 0, early)
    histories(1, VALUE1, width, early)
    histories(1, KEY1_LAST, early, wide)
    histories(1, VALUE1_LAST, width + early, wide)
    z_end(IN0)

    arrived(feat_here, recv.at[FEAT_P])
    for j in range(users):
        for t in range(tiles):
            state[tall * t + LOW * j : tall * t + LOW * (j + 1), :] = unfold(
                feat_here[j, 2 * LOW * t : 2 * LOW * (t + 1), :].astype(F32)
            )

    block_rows = 32

    def norm_state():
        def step(i, _):
            at = pl.ds(pl.multiple_of(i * block_rows, block_rows), block_rows)
            normed[at, :] = layer_norm(state[at, :]).astype(BF16)
            return 0

        lax.fori_loop(0, cands // block_rows, step, 0)

    def project(layer):
        blocks = width // wide

        def gates(j, _):
            acc = jnp.dot(normed[...], win[layer, 0, j], preferred_element_type=F32)
            at = pl.ds(pl.multiple_of(j * wide, wide), wide)
            gate[:, at] = silu_of_double(0.5 * acc)
            return 0

        lax.fori_loop(0, blocks, gates, 0)

        def others(j, _):
            acc = jnp.dot(normed[...], win[layer, 1 + j // SIDE, lax.rem(j, SIDE)], preferred_element_type=F32)
            mixed[j] = silu_of_double(0.5 * acc).astype(BF16)
            return 0

        lax.fori_loop(0, 3 * blocks, others, 0)

    scale = HEAD ** (-0.5)
    pairs = width // wide

    def attend_pair(layer, p, which):
        for i in range(wide // HEAD):
            lanes = slice(i * HEAD, (i + 1) * HEAD)
            at = pl.ds(pl.multiple_of(p * wide + i * HEAD, HEAD), HEAD)
            at_value = pl.ds(pl.multiple_of(width + p * wide + i * HEAD, HEAD), HEAD)
            past_key = kv[layer, :, at]
            past_value = kv[layer, :, at_value]
            for t in which:
                these = slice(t * tall, (t + 1) * tall)
                value = mixed[p, these, lanes]
                query = mixed[p + pairs, these, lanes]
                own_key = mixed[p + 2 * pairs, these, lanes]
                scores = lax.dot_general(
                    query, past_key, (((1,), (1,)), ((), ())), preferred_element_type=F32
                )
                weights = silu_of_double(scores * live).astype(BF16)
                total = jnp.dot(weights, past_value, preferred_element_type=F32)
                own = jnp.sum(query.astype(F32) * own_key.astype(F32), axis=-1, keepdims=True)
                own = silu_of_double(own * (0.5 * scale))
                attended[these, at] = total + own * value.astype(F32)

    def attend(layer, count):
        def step(p, _):
            attend_pair(layer, p, range(tiles))
            return 0

        lax.fori_loop(0, count, step, 0)

    def gate_and_add(layer, first, size):
        def step(i, _):
            at = pl.ds(pl.multiple_of(first + i * block_rows, block_rows), block_rows)
            normed[at, :] = (layer_norm(attended[at, :]) * gate[at, :]).astype(BF16)
            return 0

        lax.fori_loop(0, size // block_rows, step, 0)
        these = slice(first, first + size)

        def add(n, _):
            at = pl.ds(pl.multiple_of(n * wide, wide), wide)
            columns = wout[layer, n].reshape(wide, width)
            state[these, at] += lax.dot_general(
                normed[these, :], columns, (((1,), (1,)), ((), ())), preferred_element_type=F32
            )
            return 0

        lax.fori_loop(0, width // wide, add, 0)

    norm_state()
    arrived(len_in, recv.at[LEN_Z])
    length = len_in[requests[me_c]][:1, :1]
    position = lax.broadcasted_iota(jnp.int32, (1, history), 1)
    live = jnp.where(position < length, 0.5 * scale, 0.0).astype(F32)

    from_twin(IN0)
    project(0)
    z_end(WO)
    z_second(IN1)
    arrived(kv.at[0], recv.at[KV0])
    attend(0, pairs)
    from_twin(WO)
    gate_and_add(0, 0, cands)

    norm_state()
    z_end(IN1)
    from_twin(IN1)
    project(1)
    arrived(kv.at[1, :, pl.ds(0, early)], recv.at[KEY1])
    arrived(kv.at[1, :, pl.ds(width, early)], recv.at[VALUE1])
    attend(1, pairs - 1)
    arrived(kv.at[1, :, pl.ds(early, wide)], recv.at[KEY1_LAST])
    arrived(kv.at[1, :, pl.ds(width + early, wide)], recv.at[VALUE1_LAST])

    def back(t):
        for j in range(users):
            rank_out[t, j] = fold(state[tall * t + LOW * j : tall * t + LOW * (j + 1), :]).astype(BF16)
        for c in plane:
            post(rank_out.at[t, c], rank_mid[t].at[me_c], (me_s, c), send.at[RANK_P + t], recv.at[RANK_P + t])
        here(rank_out.at[t, me_c], rank_mid[t].at[me_c], recv.at[RANK_P + t])

    def home(t):
        arrived(rank_mid[t], recv.at[RANK_P + t])
        for s in range(users):
            rank_send[t, s] = rank_mid[t][inverse[s]]
        for s in column:
            post(rank_send.at[t, s], rank_in.at[t, me_s], (s, me_c), send.at[RANK_Z + t], recv.at[RANK_Z + t])
        here(rank_send.at[t, me_s], rank_in.at[t, me_s], recv.at[RANK_Z + t])

    for t in range(tiles):
        attend_pair(1, pairs - 1, (t,))
        gate_and_add(1, t * tall, tall)
        back(t)
        if t > 0:
            home(t - 1)
    home(tiles - 1)
    for t in range(tiles):
        arrived(rank_in.at[t], recv.at[RANK_Z + t])
    for m in range(users // 2):
        both = [
            unfold(rank_in[t, 2 * m + i].astype(F32)) for i in range(2) for t in range(tiles)
        ]
        out[2 * part * m : 2 * part * (m + 1), :] = jnp.concatenate(both, axis=0).astype(BF16)

    others = pl.ds(0, users - 1)
    arrived(feat_out.at[others], send.at[FEAT_Z])
    arrived(len_out.at[others], send.at[LEN_Z])
    arrived(feat_mid.at[others], send.at[FEAT_P])
    for t in range(tiles):
        arrived(rank_out.at[t, others], send.at[RANK_P + t])
        arrived(rank_send.at[t, others], send.at[RANK_Z + t])
    histories_sent(0, KV0, 0, 2 * width)
    histories_sent(1, KEY1, 0, early)
    histories_sent(1, VALUE1, width, early)
    histories_sent(1, KEY1_LAST, early, wide)
    histories_sent(1, VALUE1_LAST, width + early, wide)
    for group in (IN0, WO, IN1):
        spread_sent(group)
        z_sent(group)


def shards(kv_cache, requests, lengths, cand_feats, w_in, w_out):
    users, layers, rows, _ = kv_cache.shape
    _, part, width = cand_feats.shape
    cands, history = users * part, users * rows
    wide = w_in.shape[2]
    vmem = pl.BlockSpec(memory_space=pltpu.VMEM)
    smem = pl.BlockSpec(memory_space=pltpu.SMEM)
    anywhere = pl.BlockSpec(memory_space=pl.ANY)
    piece = pltpu.VMEM((users, 2 * part, width // 2), BF16)
    tiles = part // LOW
    tile = pltpu.VMEM((tiles, users, 2 * LOW, width // 2), BF16)
    flops = layers * (2 * cands * width * 5 * width + 4 * cands * history * width)
    ranked = pl.pallas_call(
        kernel,
        out_shape=jax.ShapeDtypeStruct((cands, width), BF16),
        in_specs=[smem, smem, anywhere, vmem, anywhere, anywhere],
        out_specs=vmem,
        scratch_shapes=[
            pltpu.VMEM((layers, SIDE, SIDE, width, wide), BF16),
            pltpu.VMEM((layers, SIDE, SIDE, width // users, width), BF16),
            pltpu.VMEM((layers, history, 2 * width), BF16),
            pltpu.VMEM((cands, width), F32),
            pltpu.VMEM((cands, width), BF16),
            pltpu.VMEM((cands, width), F32),
            pltpu.VMEM((3 * width // wide, cands, wide), BF16),
            pltpu.VMEM((cands, width), F32),
            pltpu.VMEM((users, 8, 128), jnp.int32),
            pltpu.VMEM((users, 8, 128), jnp.int32),
            *[piece] * 4,
            *[tile] * 3,
            pltpu.SMEM((users,), jnp.int32),
            pltpu.SemaphoreType.DMA((9 + 2 * tiles,)),
            pltpu.SemaphoreType.DMA((9 + 2 * tiles,)),
            pltpu.SemaphoreType.DMA((3, 2)),
            pltpu.SemaphoreType.DMA((3, 2)),
            pltpu.SemaphoreType.DMA((3, 2, 3)),
            pltpu.SemaphoreType.DMA((3, 2, 3)),
            pltpu.SemaphoreType.DMA((3, 4)),
            pltpu.SemaphoreType.DMA((3, 4)),
            pltpu.SemaphoreType.DMA((3, 5)),
            pltpu.SemaphoreType.DMA((3, 5)),
            *[pltpu.VMEM((users, 2 * LOW, width // 2), BF16)] * tiles,
        ],
        compiler_params=pltpu.CompilerParams(
            collective_id=0, has_side_effects=True, vmem_limit_bytes=60 * 1024 * 1024
        ),
        cost_estimate=pl.CostEstimate(
            flops=flops, bytes_accessed=64 * 1024 * 1024, transcendentals=cands * width * 24
        ),
        name="rank_two_layers",
    )(requests, lengths, kv_cache, cand_feats.reshape(cands, width), w_in, jnp.swapaxes(w_out, 1, 2))
    return ranked.reshape(cand_feats.shape)


def solution(mesh):
    return jax.shard_map(
        shards,
        mesh=mesh,
        in_specs=(
            P("store", None, "cand", None),
            P("store"),
            P("store"),
            P("store", "cand", None),
            P(None, None, "cand"),
            P(None, None, "cand"),
        ),
        out_specs=P("store", "cand", None),
        check_vma=False,
    )
```

```python
import functools

import jax
import jax.numpy as jnp
from jax import lax
from jax.experimental import pallas as pl
from jax.experimental.pallas import tpu as pltpu
from jax.sharding import PartitionSpec as P

MESH = pl.DeviceIdType.MESH
HEADS = 8
HEAD = 128
SIDE = 4
DEPTH = 8
LOW = 8
CORES = 2
F32 = jnp.float32
BF16 = jnp.bfloat16

PLANE = (
    ((1, 0), (3, 0), (0, 1), (0, 3))
    + ((1, 1), (3, 3), (1, 3), (3, 1))
    + ((2, 2), (2, 0), (0, 2))
    + ((2, 1), (2, 3), (1, 2), (3, 2))
)
COLUMN = tuple((dz, dk) for dz in (4, 3, 5, 2, 6, 1, 7) for dk in (0, 1)) + ((0, 1),)


def layer_norm(values):
    mean = jnp.mean(values, axis=-1, keepdims=True)
    centred = values - mean
    spread = jnp.mean(centred * centred, axis=-1, keepdims=True)
    return centred * lax.rsqrt(spread + 1e-06)


def silu_of_double(half):
    return half + half * jnp.tanh(half)


def fold(rows):
    half = rows.shape[1] // 2
    return jnp.concatenate([rows[:, :half], rows[:, half:]], axis=0)


def unfold(piece):
    half = piece.shape[0] // 2
    return jnp.concatenate([piece[:half], piece[half:]], axis=1)


def arrived(region, sem):
    pltpu.make_async_copy(region, region, sem).wait()


def kernel(
    requests,
    lengths,
    kv_hbm,
    feats,
    win_hbm,
    wout_hbm,
    out,
    win,
    wout,
    kv,
    state,
    normed,
    gate,
    mixed,
    attended,
    len_out,
    len_in,
    feat_out,
    feat_in,
    feat_mid,
    feat_here,
    rank_out,
    rank_send,
    rank_in,
    inverse,
    send,
    recv,
    a_send,
    a_recv,
    b_send,
    b_recv,
    z_send,
    z_recv,
    twin_send,
    twin_recv,
    *rank_mid,
):
    me_s = lax.axis_index("store")
    me_c = lax.axis_index("cand")
    z, core = me_s // CORES, lax.rem(me_s, CORES)
    x, y = me_c // SIDE, lax.rem(me_c, SIDE)
    layers, history, _ = kv.shape
    cands, width = state.shape
    users = kv_hbm.shape[0]
    part = cands // users
    tiles = part // LOW
    tall = users * LOW
    rows = history // users
    wide = win.shape[4]
    narrow = wout_hbm.shape[1]

    plane = [
        lax.rem(x + dx, SIDE) * SIDE + lax.rem(y + dy, SIDE) for dx, dy in PLANE
    ]
    column = [
        lax.rem(z + dz, DEPTH) * CORES + lax.rem(core + dk, CORES) for dz, dk in COLUMN
    ]
    barrier = pltpu.get_barrier_semaphore()
    for c in plane:
        pl.semaphore_signal(barrier, inc=1, device_id=(me_s, c), device_id_type=MESH)
    for s in column:
        pl.semaphore_signal(barrier, inc=1, device_id=(s, me_c), device_id_type=MESH)
    for o in range(users):
        len_out[o] = jnp.full((8, 128), lengths[o], jnp.int32)
    pl.semaphore_wait(barrier, len(plane) + len(column))

    def post(src, dst, device, send_sem, recv_sem):
        pltpu.make_async_remote_copy(
            src, dst, send_sem, recv_sem, device_id=device, device_id_type=MESH
        ).start()

    def here(src, dst, sem):
        pltpu.make_async_copy(src, dst, sem).start()

    FEAT_Z, LEN_Z, FEAT_P, KV0, KEY1, VALUE1, KEY1_LAST, VALUE1_LAST, RANK_P = range(9)
    RANK_Z = RANK_P + tiles
    early = width - wide
    IN0, WO, IN1 = range(3)

    depth = width // SIDE // CORES
    quarter = lax.rem(z, SIDE)

    def span(q, k, start=0, size=depth):
        return pl.ds(pl.multiple_of((q * CORES + k) * depth + start, size), size)

    rows_here = pl.ds(pl.multiple_of(me_c * rows, rows), rows)
    steps = (1, 3, 2)
    x_peers = [lax.rem(x + d, SIDE) * SIDE + y for d in steps]
    y_peers = [x * SIDE + lax.rem(y + d, SIDE) for d in steps]
    x_from = [lax.rem(x + SIDE - d, SIDE) for d in steps]
    y_from = [lax.rem(y + SIDE - d, SIDE) for d in steps]
    every = slice(None)

    def share(group, axis, at_x, at_y):
        if group == WO:
            low = narrow // 2
            return wout.at[:, at_x, at_y, pl.ds(axis * low, low), span(quarter, core)]
        low = depth // 2
        return win.at[group // 2, at_x, at_y, span(quarter, core, axis * low, low)]

    def source(group, axis):
        if group == WO:
            low = narrow // 2
            return wout_hbm.at[:, pl.ds(axis * low, low), span(quarter, core)]
        low = depth // 2
        return win_hbm.at[group // 2, span(quarter, core, axis * low, low)]

    def line(group, axis):
        return share(group, axis, every, y) if axis == 0 else share(group, axis, x, every)

    def spread_first(group):
        for axis, peers in enumerate((x_peers, y_peers)):
            src, dst = source(group, axis), share(group, axis, x, y)
            for c in peers:
                post(src, dst, (me_s, c), a_send.at[group, axis], a_recv.at[group, axis])
            here(src, dst, a_recv.at[group, axis])

    def spread_second(group):
        for axis, peers in enumerate((y_peers, x_peers)):
            ref = line(group, axis)
            arrived(ref, a_recv.at[group, axis])
            for i, c in enumerate(peers):
                post(ref, ref, (me_s, c), b_send.at[group, axis, i], b_recv.at[group, axis, i])

    def spread_end(group):
        for i in range(len(steps)):
            arrived(share(group, 0, every, y_from[i]), b_recv.at[group, 0, i])
            arrived(share(group, 1, x_from[i], every), b_recv.at[group, 1, i])

    def spread_sent(group):
        most = pl.ds(0, SIDE - 1)
        arrived(share(group, 0, most, y), a_send.at[group, 0])
        arrived(share(group, 1, x, most), a_send.at[group, 1])
        for i in range(len(steps)):
            arrived(line(group, 0), b_send.at[group, 0, i])
            arrived(line(group, 1), b_send.at[group, 1, i])

    def histories(layer, number, first, size):
        lanes = pl.ds(first, size)
        dst = kv.at[layer, rows_here, lanes]
        for c in plane:
            src = kv_hbm.at[c, layer, :, lanes]
            post(src, dst, (me_s, c), send.at[number], recv.at[number])
        here(kv_hbm.at[me_c, layer, :, lanes], dst, recv.at[number])

    def histories_sent(layer, number, first, size):
        lanes = pl.ds(first, size)
        arrived(kv.at[layer, pl.ds(0, (users - 1) * rows), lanes], send.at[number])

    up, down = lax.rem(z + 1, DEPTH) * CORES, lax.rem(z + DEPTH - 1, DEPTH) * CORES
    twin = z * CORES + 1 - core
    ahead, behind, across = (lax.rem(quarter + d, SIDE) for d in (1, 3, 2))
    low, high = pl.ds(0, SIDE // 2), pl.ds(SIDE // 2, SIDE // 2)

    def block(group, q, k, part_of=every):
        if group == WO:
            return wout.at[:, part_of, :, :, span(q, k)]
        return win.at[group // 2, part_of, :, span(q, k)]

    def along(ref, to, group, i):
        post(ref, ref, (to + core, me_c), z_send.at[group, i], z_recv.at[group, i])

    def to_twin(ref, group, i):
        post(ref, ref, (twin, me_c), twin_send.at[group, i], twin_recv.at[group, i])

    def z_first(group):
        ref = block(group, quarter, core)
        along(ref, up, group, 0)
        along(ref, down, group, 1)
        to_twin(ref, group, 0)

    def z_second(group):
        for i, (q, to, part_of) in enumerate(((behind, up, low), (ahead, down, high))):
            arrived(block(group, q, core), z_recv.at[group, i])
            along(block(group, q, core, part_of), to, group, 2 + i)
            to_twin(block(group, q, core), group, 1 + i)

    def z_end(group):
        for i, part_of in enumerate((low, high)):
            ref = block(group, across, core, part_of)
            arrived(ref, z_recv.at[group, 2 + i])
            to_twin(ref, group, 3 + i)

    def from_twin(group):
        for i, (q, part_of) in enumerate(
            ((quarter, every), (behind, every), (ahead, every), (across, low), (across, high))
        ):
            arrived(block(group, q, 1 - core, part_of), twin_recv.at[group, i])

    def z_sent(group):
        whole, part_of = block(group, quarter, core), block(group, quarter, core, low)
        for i in range(4):
            arrived(whole if i < 2 else part_of, z_send.at[group, i])
        for i in range(5):
            arrived(whole if i < 3 else part_of, twin_send.at[group, i])

    spread_first(IN0)
    spread_first(WO)

    for m in range(users // 2):
        both = feats[2 * part * m : 2 * part * (m + 1), :].astype(F32)
        for i in range(2):
            for t in range(tiles):
                first = part * i + LOW * t
                feat_out[2 * m + i, 2 * LOW * t : 2 * LOW * (t + 1), :] = fold(
                    both[first : first + LOW]
                ).astype(BF16)
    for s in column:
        post(feat_out.at[s], feat_in.at[me_s], (s, me_c), send.at[FEAT_Z], recv.at[FEAT_Z])
    here(feat_out.at[me_s], feat_in.at[me_s], recv.at[FEAT_Z])
    for s in column:
        post(len_out.at[s], len_in.at[me_s], (s, me_c), send.at[LEN_Z], recv.at[LEN_Z])
    here(len_out.at[me_s], len_in.at[me_s], recv.at[LEN_Z])

    spread_second(IN0)
    spread_first(IN1)
    spread_second(WO)
    spread_end(IN0)
    z_first(IN0)
    spread_second(IN1)
    spread_end(WO)
    z_first(WO)
    spread_end(IN1)

    for first in (0, width):
        histories(0, KV0, first, width // 2)
    arrived(feat_in, recv.at[FEAT_Z])
    for k in range(users):
        feat_mid[k] = feat_in[requests[k]]
    for c in plane:
        post(feat_mid.at[c], feat_here.at[me_c], (me_s, c), send.at[FEAT_P], recv.at[FEAT_P])
    here(feat_mid.at[me_c], feat_here.at[me_c], recv.at[FEAT_P])

    for first in (width // 2, width + width // 2):
        histories(0, KV0, first, width // 2)

    for s in range(users):
        at = 0
        for k in range(users):
            at = jnp.where(requests[k] == s, k, at)
        inverse[s] = at

    z_second(IN0)
    z_first(IN1)
    z_second(WO)
    histories(1, KEY1, 0, early)
    histories(1, VALUE1, width, early)
    histories(1, KEY1_LAST, early, wide)
    histories(1, VALUE1_LAST, width + early, wide)
    z_end(IN0)

    arrived(feat_here, recv.at[FEAT_P])
    for j in range(users):
        for t in range(tiles):
            state[tall * t + LOW * j : tall * t + LOW * (j + 1), :] = unfold(
                feat_here[j, 2 * LOW * t : 2 * LOW * (t + 1), :].astype(F32)
            )

    block_rows = 32

    def norm_state():
        def step(i, _):
            at = pl.ds(pl.multiple_of(i * block_rows, block_rows), block_rows)
            normed[at, :] = layer_norm(state[at, :]).astype(BF16)
            return 0

        lax.fori_loop(0, cands // block_rows, step, 0)

    def project(layer):
        blocks = width // wide

        def gates(j, _):
            acc = jnp.dot(normed[...], win[layer, 0, j], preferred_element_type=F32)
            at = pl.ds(pl.multiple_of(j * wide, wide), wide)
            gate[:, at] = silu_of_double(0.5 * acc)
            return 0

        lax.fori_loop(0, blocks, gates, 0)

        def others(j, _):
            acc = jnp.dot(normed[...], win[layer, 1 + j // SIDE, lax.rem(j, SIDE)], preferred_element_type=F32)
            mixed[j] = silu_of_double(0.5 * acc).astype(BF16)
            return 0

        lax.fori_loop(0, 3 * blocks, others, 0)

    scale = HEAD ** (-0.5)
    pairs = width // wide

    def attend_pair(layer, p, which):
        for i in range(wide // HEAD):
            lanes = slice(i * HEAD, (i + 1) * HEAD)
            at = pl.ds(pl.multiple_of(p * wide + i * HEAD, HEAD), HEAD)
            at_value = pl.ds(pl.multiple_of(width + p * wide + i * HEAD, HEAD), HEAD)
            past_key = kv[layer, :, at]
            past_value = kv[layer, :, at_value]
            for t in which:
                these = slice(t * tall, (t + 1) * tall)
                value = mixed[p, these, lanes]
                query = mixed[p + pairs, these, lanes]
                own_key = mixed[p + 2 * pairs, these, lanes]
                scores = lax.dot_general(
                    query, past_key, (((1,), (1,)), ((), ())), preferred_element_type=F32
                )
                weights = silu_of_double(scores * live).astype(BF16)
                total = jnp.dot(weights, past_value, preferred_element_type=F32)
                own = jnp.sum(query.astype(F32) * own_key.astype(F32), axis=-1, keepdims=True)
                own = silu_of_double(own * (0.5 * scale))
                attended[these, at] = total + own * value.astype(F32)

    def attend(layer, count):
        def step(p, _):
            attend_pair(layer, p, range(tiles))
            return 0

        lax.fori_loop(0, count, step, 0)

    def gate_and_add(layer, first, size):
        def step(i, _):
            at = pl.ds(pl.multiple_of(first + i * block_rows, block_rows), block_rows)
            normed[at, :] = (layer_norm(attended[at, :]) * gate[at, :]).astype(BF16)
            return 0

        lax.fori_loop(0, size // block_rows, step, 0)
        these = slice(first, first + size)

        def add(n, _):
            at = pl.ds(pl.multiple_of(n * wide, wide), wide)
            columns = wout[layer, n].reshape(wide, width)
            state[these, at] += lax.dot_general(
                normed[these, :], columns, (((1,), (1,)), ((), ())), preferred_element_type=F32
            )
            return 0

        lax.fori_loop(0, width // wide, add, 0)

    norm_state()
    arrived(len_in, recv.at[LEN_Z])
    length = len_in[requests[me_c]][:1, :1]
    position = lax.broadcasted_iota(jnp.int32, (1, history), 1)
    live = jnp.where(position < length, 0.5 * scale, 0.0).astype(F32)

    from_twin(IN0)
    project(0)
    z_end(WO)
    z_second(IN1)
    arrived(kv.at[0], recv.at[KV0])
    attend(0, pairs)
    from_twin(WO)
    gate_and_add(0, 0, cands)

    norm_state()
    z_end(IN1)
    from_twin(IN1)
    project(1)
    arrived(kv.at[1, :, pl.ds(0, early)], recv.at[KEY1])
    arrived(kv.at[1, :, pl.ds(width, early)], recv.at[VALUE1])
    attend(1, pairs - 1)
    arrived(kv.at[1, :, pl.ds(early, wide)], recv.at[KEY1_LAST])
    arrived(kv.at[1, :, pl.ds(width + early, wide)], recv.at[VALUE1_LAST])

    def back(t):
        for j in range(users):
            rank_out[t, j] = fold(state[tall * t + LOW * j : tall * t + LOW * (j + 1), :]).astype(BF16)
        for c in plane:
            post(rank_out.at[t, c], rank_mid[t].at[me_c], (me_s, c), send.at[RANK_P + t], recv.at[RANK_P + t])
        here(rank_out.at[t, me_c], rank_mid[t].at[me_c], recv.at[RANK_P + t])

    def home(t):
        arrived(rank_mid[t], recv.at[RANK_P + t])
        for s in range(users):
            rank_send[t, s] = rank_mid[t][inverse[s]]
        for s in column:
            post(rank_send.at[t, s], rank_in.at[t, me_s], (s, me_c), send.at[RANK_Z + t], recv.at[RANK_Z + t])
        here(rank_send.at[t, me_s], rank_in.at[t, me_s], recv.at[RANK_Z + t])

    for t in range(tiles):
        attend_pair(1, pairs - 1, (t,))
        gate_and_add(1, t * tall, tall)
        back(t)
        if t > 0:
            home(t - 1)
    home(tiles - 1)
    for t in range(tiles):
        arrived(rank_in.at[t], recv.at[RANK_Z + t])
    for m in range(users // 2):
        both = [
            unfold(rank_in[t, 2 * m + i].astype(F32)) for i in range(2) for t in range(tiles)
        ]
        out[2 * part * m : 2 * part * (m + 1), :] = jnp.concatenate(both, axis=0).astype(BF16)

    others = pl.ds(0, users - 1)
    arrived(feat_out.at[others], send.at[FEAT_Z])
    arrived(len_out.at[others], send.at[LEN_Z])
    arrived(feat_mid.at[others], send.at[FEAT_P])
    for t in range(tiles):
        arrived(rank_out.at[t, others], send.at[RANK_P + t])
        arrived(rank_send.at[t, others], send.at[RANK_Z + t])
    histories_sent(0, KV0, 0, 2 * width)
    histories_sent(1, KEY1, 0, early)
    histories_sent(1, VALUE1, width, early)
    histories_sent(1, KEY1_LAST, early, wide)
    histories_sent(1, VALUE1_LAST, width + early, wide)
    for group in (IN0, WO, IN1):
        spread_sent(group)
        z_sent(group)


def shards(kv_cache, requests, lengths, cand_feats, w_in, w_out):
    users, layers, rows, _ = kv_cache.shape
    _, part, width = cand_feats.shape
    cands, history = users * part, users * rows
    wide = w_in.shape[2]
    vmem = pl.BlockSpec(memory_space=pltpu.VMEM)
    smem = pl.BlockSpec(memory_space=pltpu.SMEM)
    anywhere = pl.BlockSpec(memory_space=pl.ANY)
    piece = pltpu.VMEM((users, 2 * part, width // 2), BF16)
    tiles = part // LOW
    tile = pltpu.VMEM((tiles, users, 2 * LOW, width // 2), BF16)
    flops = layers * (2 * cands * width * 5 * width + 4 * cands * history * width)
    ranked = pl.pallas_call(
        kernel,
        out_shape=jax.ShapeDtypeStruct((cands, width), BF16),
        in_specs=[smem, smem, anywhere, vmem, anywhere, anywhere],
        out_specs=vmem,
        scratch_shapes=[
            pltpu.VMEM((layers, SIDE, SIDE, width, wide), BF16),
            pltpu.VMEM((layers, SIDE, SIDE, width // users, width), BF16),
            pltpu.VMEM((layers, history, 2 * width), BF16),
            pltpu.VMEM((cands, width), F32),
            pltpu.VMEM((cands, width), BF16),
            pltpu.VMEM((cands, width), F32),
            pltpu.VMEM((3 * width // wide, cands, wide), BF16),
            pltpu.VMEM((cands, width), F32),
            pltpu.VMEM((users, 8, 128), jnp.int32),
            pltpu.VMEM((users, 8, 128), jnp.int32),
            *[piece] * 4,
            *[tile] * 3,
            pltpu.SMEM((users,), jnp.int32),
            pltpu.SemaphoreType.DMA((9 + 2 * tiles,)),
            pltpu.SemaphoreType.DMA((9 + 2 * tiles,)),
            pltpu.SemaphoreType.DMA((3, 2)),
            pltpu.SemaphoreType.DMA((3, 2)),
            pltpu.SemaphoreType.DMA((3, 2, 3)),
            pltpu.SemaphoreType.DMA((3, 2, 3)),
            pltpu.SemaphoreType.DMA((3, 4)),
            pltpu.SemaphoreType.DMA((3, 4)),
            pltpu.SemaphoreType.DMA((3, 5)),
            pltpu.SemaphoreType.DMA((3, 5)),
            *[pltpu.VMEM((users, 2 * LOW, width // 2), BF16)] * tiles,
        ],
        compiler_params=pltpu.CompilerParams(
            collective_id=0, has_side_effects=True, vmem_limit_bytes=60 * 1024 * 1024
        ),
        cost_estimate=pl.CostEstimate(
            flops=flops, bytes_accessed=64 * 1024 * 1024, transcendentals=cands * width * 24
        ),
        name="rank_two_layers",
    )(requests, lengths, kv_cache, cand_feats.reshape(cands, width), w_in, jnp.swapaxes(w_out, 1, 2))
    return ranked.reshape(cand_feats.shape)


def solution(mesh):
    return jax.shard_map(
        shards,
        mesh=mesh,
        in_specs=(
            P("store", None, "cand", None),
            P("store"),
            P("store"),
            P("store", "cand", None),
            P(None, None, "cand"),
            P(None, None, "cand"),
        ),
        out_specs=P("store", "cand", None),
        check_vma=False,
    )
```

```python
import functools

import jax
import jax.numpy as jnp
from jax import lax
from jax.experimental import pallas as pl
from jax.experimental.pallas import tpu as pltpu
from jax.sharding import PartitionSpec as P

MESH = pl.DeviceIdType.MESH
HEADS = 8
HEAD = 128
SIDE = 4
DEPTH = 8
LOW = 8
CORES = 2
F32 = jnp.float32
BF16 = jnp.bfloat16

PLANE = (
    ((1, 0), (3, 0), (0, 1), (0, 3))
    + ((1, 1), (3, 3), (1, 3), (3, 1))
    + ((2, 2), (2, 0), (0, 2))
    + ((2, 1), (2, 3), (1, 2), (3, 2))
)
COLUMN = tuple((dz, dk) for dz in (4, 3, 5, 2, 6, 1, 7) for dk in (0, 1)) + ((0, 1),)


def layer_norm(values):
    mean = jnp.mean(values, axis=-1, keepdims=True)
    centred = values - mean
    spread = jnp.mean(centred * centred, axis=-1, keepdims=True)
    return centred * lax.rsqrt(spread + 1e-06)


def silu_of_double(half):
    return half + half * jnp.tanh(half)


def fold(rows):
    half = rows.shape[1] // 2
    return jnp.concatenate([rows[:, :half], rows[:, half:]], axis=0)


def unfold(piece):
    half = piece.shape[0] // 2
    return jnp.concatenate([piece[:half], piece[half:]], axis=1)


def arrived(region, sem):
    pltpu.make_async_copy(region, region, sem).wait()


def kernel(
    requests,
    lengths,
    kv_hbm,
    feats_hbm,
    win_hbm,
    wout_hbm,
    out,
    win,
    wout,
    kv,
    state,
    normed,
    gate,
    mixed,
    attended,
    len_out,
    len_in,
    feat_out,
    feat_in,
    feat_mid,
    feat_here,
    rank_out,
    rank_send,
    rank_in,
    inverse,
    send,
    recv,
    a_send,
    a_recv,
    b_send,
    b_recv,
    z_send,
    z_recv,
    twin_send,
    twin_recv,
    feats,
    feats_sem,
    *rank_mid,
):
    me_s = lax.axis_index("store")
    me_c = lax.axis_index("cand")
    z, core = me_s // CORES, lax.rem(me_s, CORES)
    x, y = me_c // SIDE, lax.rem(me_c, SIDE)
    layers, history, _ = kv.shape
    cands, width = state.shape
    users = kv_hbm.shape[0]
    part = cands // users
    tiles = part // LOW
    tall = users * LOW
    rows = history // users
    wide = win.shape[4]
    narrow = wout_hbm.shape[1]

    plane = [
        lax.rem(x + dx, SIDE) * SIDE + lax.rem(y + dy, SIDE) for dx, dy in PLANE
    ]
    column = [
        lax.rem(z + dz, DEPTH) * CORES + lax.rem(core + dk, CORES) for dz, dk in COLUMN
    ]
    feats_copy = pltpu.make_async_copy(feats_hbm, feats, feats_sem)
    feats_copy.start()
    barrier = pltpu.get_barrier_semaphore()
    for c in plane:
        pl.semaphore_signal(barrier, inc=1, device_id=(me_s, c), device_id_type=MESH)
    for s in column:
        pl.semaphore_signal(barrier, inc=1, device_id=(s, me_c), device_id_type=MESH)
    for o in range(users):
        len_out[o] = jnp.full((8, 128), lengths[o], jnp.int32)
    pl.semaphore_wait(barrier, len(plane) + len(column))

    def post(src, dst, device, send_sem, recv_sem):
        pltpu.make_async_remote_copy(
            src, dst, send_sem, recv_sem, device_id=device, device_id_type=MESH
        ).start()

    def here(src, dst, sem):
        pltpu.make_async_copy(src, dst, sem).start()

    FEAT_Z, LEN_Z, FEAT_P, KV0, KEY1, VALUE1, KEY1_LAST, VALUE1_LAST, RANK_P = range(9)
    RANK_Z = RANK_P + tiles
    early = width - wide
    IN0, WO, IN1 = range(3)

    depth = width // SIDE // CORES
    quarter = lax.rem(z, SIDE)

    def span(q, k, start=0, size=depth):
        return pl.ds(pl.multiple_of((q * CORES + k) * depth + start, size), size)

    rows_here = pl.ds(pl.multiple_of(me_c * rows, rows), rows)
    steps = (1, 3, 2)
    x_peers = [lax.rem(x + d, SIDE) * SIDE + y for d in steps]
    y_peers = [x * SIDE + lax.rem(y + d, SIDE) for d in steps]
    x_from = [lax.rem(x + SIDE - d, SIDE) for d in steps]
    y_from = [lax.rem(y + SIDE - d, SIDE) for d in steps]
    every = slice(None)

    def share(group, axis, at_x, at_y):
        if group == WO:
            low = narrow // 2
            return wout.at[:, at_x, at_y, pl.ds(axis * low, low), span(quarter, core)]
        low = depth // 2
        return win.at[group // 2, at_x, at_y, span(quarter, core, axis * low, low)]

    def source(group, axis):
        if group == WO:
            low = narrow // 2
            return wout_hbm.at[:, pl.ds(axis * low, low), span(quarter, core)]
        low = depth // 2
        return win_hbm.at[group // 2, span(quarter, core, axis * low, low)]

    def line(group, axis):
        return share(group, axis, every, y) if axis == 0 else share(group, axis, x, every)

    def spread_first(group):
        for axis, peers in enumerate((x_peers, y_peers)):
            src, dst = source(group, axis), share(group, axis, x, y)
            for c in peers:
                post(src, dst, (me_s, c), a_send.at[group, axis], a_recv.at[group, axis])
            here(src, dst, a_recv.at[group, axis])

    def spread_second(group):
        for axis, peers in enumerate((y_peers, x_peers)):
            ref = line(group, axis)
            arrived(ref, a_recv.at[group, axis])
            for i, c in enumerate(peers):
                post(ref, ref, (me_s, c), b_send.at[group, axis, i], b_recv.at[group, axis, i])

    def spread_end(group):
        for i in range(len(steps)):
            arrived(share(group, 0, every, y_from[i]), b_recv.at[group, 0, i])
            arrived(share(group, 1, x_from[i], every), b_recv.at[group, 1, i])

    def spread_sent(group):
        most = pl.ds(0, SIDE - 1)
        arrived(share(group, 0, most, y), a_send.at[group, 0])
        arrived(share(group, 1, x, most), a_send.at[group, 1])
        for i in range(len(steps)):
            arrived(line(group, 0), b_send.at[group, 0, i])
            arrived(line(group, 1), b_send.at[group, 1, i])

    def histories(layer, number, first, size):
        lanes = pl.ds(first, size)
        dst = kv.at[layer, rows_here, lanes]
        for c in plane:
            src = kv_hbm.at[c, layer, :, lanes]
            post(src, dst, (me_s, c), send.at[number], recv.at[number])
        here(kv_hbm.at[me_c, layer, :, lanes], dst, recv.at[number])

    def histories_sent(layer, number, first, size):
        lanes = pl.ds(first, size)
        arrived(kv.at[layer, pl.ds(0, (users - 1) * rows), lanes], send.at[number])

    up, down = lax.rem(z + 1, DEPTH) * CORES, lax.rem(z + DEPTH - 1, DEPTH) * CORES
    twin = z * CORES + 1 - core
    ahead, behind, across = (lax.rem(quarter + d, SIDE) for d in (1, 3, 2))
    low, high = pl.ds(0, SIDE // 2), pl.ds(SIDE // 2, SIDE // 2)

    def block(group, q, k, part_of=every):
        if group == WO:
            return wout.at[:, part_of, :, :, span(q, k)]
        return win.at[group // 2, part_of, :, span(q, k)]

    def along(ref, to, group, i):
        post(ref, ref, (to + core, me_c), z_send.at[group, i], z_recv.at[group, i])

    def to_twin(ref, group, i):
        post(ref, ref, (twin, me_c), twin_send.at[group, i], twin_recv.at[group, i])

    def z_first(group):
        ref = block(group, quarter, core)
        along(ref, up, group, 0)
        along(ref, down, group, 1)
        to_twin(ref, group, 0)

    def z_second(group):
        for i, (q, to, part_of) in enumerate(((behind, up, low), (ahead, down, high))):
            arrived(block(group, q, core), z_recv.at[group, i])
            along(block(group, q, core, part_of), to, group, 2 + i)
            to_twin(block(group, q, core), group, 1 + i)

    def z_end(group):
        for i, part_of in enumerate((low, high)):
            ref = block(group, across, core, part_of)
            arrived(ref, z_recv.at[group, 2 + i])
            to_twin(ref, group, 3 + i)

    def from_twin(group):
        for i, (q, part_of) in enumerate(
            ((quarter, every), (behind, every), (ahead, every), (across, low), (across, high))
        ):
            arrived(block(group, q, 1 - core, part_of), twin_recv.at[group, i])

    def z_sent(group):
        whole, part_of = block(group, quarter, core), block(group, quarter, core, low)
        for i in range(4):
            arrived(whole if i < 2 else part_of, z_send.at[group, i])
        for i in range(5):
            arrived(whole if i < 3 else part_of, twin_send.at[group, i])

    spread_first(IN0)
    spread_first(WO)

    feats_copy.wait()
    for m in range(users // 2):
        both = feats[2 * part * m : 2 * part * (m + 1), :].astype(F32)
        for i in range(2):
            for t in range(tiles):
                first = part * i + LOW * t
                feat_out[2 * m + i, 2 * LOW * t : 2 * LOW * (t + 1), :] = fold(
                    both[first : first + LOW]
                ).astype(BF16)
    for s in column:
        post(feat_out.at[s], feat_in.at[me_s], (s, me_c), send.at[FEAT_Z], recv.at[FEAT_Z])
    here(feat_out.at[me_s], feat_in.at[me_s], recv.at[FEAT_Z])
    for s in column:
        post(len_out.at[s], len_in.at[me_s], (s, me_c), send.at[LEN_Z], recv.at[LEN_Z])
    here(len_out.at[me_s], len_in.at[me_s], recv.at[LEN_Z])

    spread_second(IN0)
    spread_first(IN1)
    spread_second(WO)
    spread_end(IN0)
    z_first(IN0)
    spread_second(IN1)
    spread_end(WO)
    z_first(WO)
    spread_end(IN1)

    for first in (0, width):
        histories(0, KV0, first, width // 2)
    arrived(feat_in, recv.at[FEAT_Z])
    for k in range(users):
        feat_mid[k] = feat_in[requests[k]]
    for c in plane:
        post(feat_mid.at[c], feat_here.at[me_c], (me_s, c), send.at[FEAT_P], recv.at[FEAT_P])
    here(feat_mid.at[me_c], feat_here.at[me_c], recv.at[FEAT_P])

    for first in (width // 2, width + width // 2):
        histories(0, KV0, first, width // 2)

    for s in range(users):
        at = 0
        for k in range(users):
            at = jnp.where(requests[k] == s, k, at)
        inverse[s] = at

    z_second(IN0)
    z_first(IN1)
    z_second(WO)
    histories(1, KEY1, 0, early)
    histories(1, VALUE1, width, early)
    histories(1, KEY1_LAST, early, wide)
    histories(1, VALUE1_LAST, width + early, wide)
    z_end(IN0)

    arrived(feat_here, recv.at[FEAT_P])
    for j in range(users):
        for t in range(tiles):
            state[tall * t + LOW * j : tall * t + LOW * (j + 1), :] = unfold(
                feat_here[j, 2 * LOW * t : 2 * LOW * (t + 1), :].astype(F32)
            )

    block_rows = 32

    def norm_state():
        def step(i, _):
            at = pl.ds(pl.multiple_of(i * block_rows, block_rows), block_rows)
            normed[at, :] = layer_norm(state[at, :]).astype(BF16)
            return 0

        lax.fori_loop(0, cands // block_rows, step, 0)

    def project(layer):
        blocks = width // wide

        def gates(j, _):
            acc = jnp.dot(normed[...], win[layer, 0, j], preferred_element_type=F32)
            at = pl.ds(pl.multiple_of(j * wide, wide), wide)
            gate[:, at] = silu_of_double(0.5 * acc)
            return 0

        lax.fori_loop(0, blocks, gates, 0)

        def others(j, _):
            acc = jnp.dot(normed[...], win[layer, 1 + j // SIDE, lax.rem(j, SIDE)], preferred_element_type=F32)
            mixed[j] = silu_of_double(0.5 * acc).astype(BF16)
            return 0

        lax.fori_loop(0, 3 * blocks, others, 0)

    scale = HEAD ** (-0.5)
    pairs = width // wide

    def attend_pair(layer, p, which):
        for i in range(wide // HEAD):
            lanes = slice(i * HEAD, (i + 1) * HEAD)
            at = pl.ds(pl.multiple_of(p * wide + i * HEAD, HEAD), HEAD)
            at_value = pl.ds(pl.multiple_of(width + p * wide + i * HEAD, HEAD), HEAD)
            past_key = kv[layer, :, at]
            past_value = kv[layer, :, at_value]
            for t in which:
                these = slice(t * tall, (t + 1) * tall)
                value = mixed[p, these, lanes]
                query = mixed[p + pairs, these, lanes]
                own_key = mixed[p + 2 * pairs, these, lanes]
                scores = lax.dot_general(
                    query, past_key, (((1,), (1,)), ((), ())), preferred_element_type=F32
                )
                weights = silu_of_double(scores * live).astype(BF16)
                total = jnp.dot(weights, past_value, preferred_element_type=F32)
                own = jnp.sum(query.astype(F32) * own_key.astype(F32), axis=-1, keepdims=True)
                own = silu_of_double(own * (0.5 * scale))
                attended[these, at] = total + own * value.astype(F32)

    def attend(layer, count):
        def step(p, _):
            attend_pair(layer, p, range(tiles))
            return 0

        lax.fori_loop(0, count, step, 0)

    def gate_and_add(layer, first, size):
        def step(i, _):
            at = pl.ds(pl.multiple_of(first + i * block_rows, block_rows), block_rows)
            normed[at, :] = (layer_norm(attended[at, :]) * gate[at, :]).astype(BF16)
            return 0

        lax.fori_loop(0, size // block_rows, step, 0)
        these = slice(first, first + size)

        def add(n, _):
            at = pl.ds(pl.multiple_of(n * wide, wide), wide)
            columns = wout[layer, n].reshape(wide, width)
            state[these, at] += lax.dot_general(
                normed[these, :], columns, (((1,), (1,)), ((), ())), preferred_element_type=F32
            )
            return 0

        lax.fori_loop(0, width // wide, add, 0)

    norm_state()
    arrived(len_in, recv.at[LEN_Z])
    length = len_in[requests[me_c]][:1, :1]
    position = lax.broadcasted_iota(jnp.int32, (1, history), 1)
    live = jnp.where(position < length, 0.5 * scale, 0.0).astype(F32)

    from_twin(IN0)
    project(0)
    z_end(WO)
    z_second(IN1)
    arrived(kv.at[0], recv.at[KV0])
    attend(0, pairs)
    from_twin(WO)
    gate_and_add(0, 0, cands)

    norm_state()
    z_end(IN1)
    from_twin(IN1)
    project(1)
    arrived(kv.at[1, :, pl.ds(0, early)], recv.at[KEY1])
    arrived(kv.at[1, :, pl.ds(width, early)], recv.at[VALUE1])
    attend(1, pairs - 1)
    arrived(kv.at[1, :, pl.ds(early, wide)], recv.at[KEY1_LAST])
    arrived(kv.at[1, :, pl.ds(width + early, wide)], recv.at[VALUE1_LAST])

    def back(t):
        for j in range(users):
            rank_out[t, j] = fold(state[tall * t + LOW * j : tall * t + LOW * (j + 1), :]).astype(BF16)
        for c in plane:
            post(rank_out.at[t, c], rank_mid[t].at[me_c], (me_s, c), send.at[RANK_P + t], recv.at[RANK_P + t])
        here(rank_out.at[t, me_c], rank_mid[t].at[me_c], recv.at[RANK_P + t])

    def home(t):
        arrived(rank_mid[t], recv.at[RANK_P + t])
        for s in range(users):
            rank_send[t, s] = rank_mid[t][inverse[s]]
        for s in column:
            post(rank_send.at[t, s], rank_in.at[t, me_s], (s, me_c), send.at[RANK_Z + t], recv.at[RANK_Z + t])
        here(rank_send.at[t, me_s], rank_in.at[t, me_s], recv.at[RANK_Z + t])

    for t in range(tiles):
        attend_pair(1, pairs - 1, (t,))
        gate_and_add(1, t * tall, tall)
        back(t)
        if t > 0:
            home(t - 1)
    home(tiles - 1)
    for t in range(tiles):
        arrived(rank_in.at[t], recv.at[RANK_Z + t])
        for o in range(users):
            first = part * o + LOW * t
            state[first : first + LOW, :] = unfold(rank_in[t, o].astype(F32))

    def cast(i, _):
        at = pl.ds(pl.multiple_of(i * block_rows, block_rows), block_rows)
        out[at, :] = state[at, :].astype(BF16)
        return 0

    lax.fori_loop(0, cands // block_rows, cast, 0)

    others = pl.ds(0, users - 1)
    arrived(feat_out.at[others], send.at[FEAT_Z])
    arrived(len_out.at[others], send.at[LEN_Z])
    arrived(feat_mid.at[others], send.at[FEAT_P])
    for t in range(tiles):
        arrived(rank_out.at[t, others], send.at[RANK_P + t])
        arrived(rank_send.at[t, others], send.at[RANK_Z + t])
    histories_sent(0, KV0, 0, 2 * width)
    histories_sent(1, KEY1, 0, early)
    histories_sent(1, VALUE1, width, early)
    histories_sent(1, KEY1_LAST, early, wide)
    histories_sent(1, VALUE1_LAST, width + early, wide)
    for group in (IN0, WO, IN1):
        spread_sent(group)
        z_sent(group)


def shards(kv_cache, requests, lengths, cand_feats, w_in, w_out):
    users, layers, rows, _ = kv_cache.shape
    _, part, width = cand_feats.shape
    cands, history = users * part, users * rows
    wide = w_in.shape[2]
    vmem = pl.BlockSpec(memory_space=pltpu.VMEM)
    smem = pl.BlockSpec(memory_space=pltpu.SMEM)
    anywhere = pl.BlockSpec(memory_space=pl.ANY)
    piece = pltpu.VMEM((users, 2 * part, width // 2), BF16)
    tiles = part // LOW
    tile = pltpu.VMEM((tiles, users, 2 * LOW, width // 2), BF16)
    flops = layers * (2 * cands * width * 5 * width + 4 * cands * history * width)
    ranked = pl.pallas_call(
        kernel,
        out_shape=jax.ShapeDtypeStruct((cands, width), BF16),
        in_specs=[smem, smem, anywhere, anywhere, anywhere, anywhere],
        out_specs=vmem,
        scratch_shapes=[
            pltpu.VMEM((layers, SIDE, SIDE, width, wide), BF16),
            pltpu.VMEM((layers, SIDE, SIDE, width // users, width), BF16),
            pltpu.VMEM((layers, history, 2 * width), BF16),
            pltpu.VMEM((cands, width), F32),
            pltpu.VMEM((cands, width), BF16),
            pltpu.VMEM((cands, width), F32),
            pltpu.VMEM((3 * width // wide, cands, wide), BF16),
            pltpu.VMEM((cands, width), F32),
            pltpu.VMEM((users, 8, 128), jnp.int32),
            pltpu.VMEM((users, 8, 128), jnp.int32),
            *[piece] * 4,
            *[tile] * 3,
            pltpu.SMEM((users,), jnp.int32),
            pltpu.SemaphoreType.DMA((9 + 2 * tiles,)),
            pltpu.SemaphoreType.DMA((9 + 2 * tiles,)),
            pltpu.SemaphoreType.DMA((3, 2)),
            pltpu.SemaphoreType.DMA((3, 2)),
            pltpu.SemaphoreType.DMA((3, 2, 3)),
            pltpu.SemaphoreType.DMA((3, 2, 3)),
            pltpu.SemaphoreType.DMA((3, 4)),
            pltpu.SemaphoreType.DMA((3, 4)),
            pltpu.SemaphoreType.DMA((3, 5)),
            pltpu.SemaphoreType.DMA((3, 5)),
            pltpu.VMEM((cands, width), BF16),
            pltpu.SemaphoreType.DMA,
            *[pltpu.VMEM((users, 2 * LOW, width // 2), BF16)] * tiles,
        ],
        compiler_params=pltpu.CompilerParams(
            collective_id=0, has_side_effects=True, vmem_limit_bytes=60 * 1024 * 1024
        ),
        cost_estimate=pl.CostEstimate(
            flops=flops, bytes_accessed=64 * 1024 * 1024, transcendentals=cands * width * 24
        ),
        name="rank_two_layers",
    )(requests, lengths, kv_cache, cand_feats.reshape(cands, width), w_in, jnp.swapaxes(w_out, 1, 2))
    return ranked.reshape(cand_feats.shape)


def solution(mesh):
    return jax.shard_map(
        shards,
        mesh=mesh,
        in_specs=(
            P("store", None, "cand", None),
            P("store"),
            P("store"),
            P("store", "cand", None),
            P(None, None, "cand"),
            P(None, None, "cand"),
        ),
        out_specs=P("store", "cand", None),
        check_vma=False,
    )
```
